32 devices in a mesh: panel: 8 (over y, x, core), group: 4 (over z).
Axes of the slice: x: 2, y: 2, z: 4, core: 2. Of those that a mesh axis runs over, the one named last changes fastest.
Arguments:
- displacement: bfloat16 [96, 524288], P(None, ('panel', 'group')), may hold values from -6 to 6
- send_index: int32 [32, 16384], P(('panel', 'group')), may hold values from 0 to 16383, each once within a row
- support: int32 [32, 16384], P(('panel', 'group')), may hold values from 0 to 16383, each once within a row
- support_xyz: float32 [3, 524288], P(None, ('panel', 'group')), may hold values from -1.1 to 1.1, as said below
- patch_kernel_inverse: bfloat16 [64, 64, 8192], P('group', None, 'panel'), may hold values from -0.75 to 0.75
- panel_xyz: float32 [3, 65536], P(None, ('panel', 'group')), may hold values from -1.1 to 1.1, as said below
- normals: float32 [3, 65536], P(None, ('panel', 'group')), may hold values from -3 to 3
- centers: float32 [3, 8192], P(None, ('panel', 'group')), may hold values from -1 to 1
- member: int32 [65536], P(('panel', 'group')), may hold values from 0 to 255
Outputs:
- normal_velocity: float32 [32, 65536], P(None, ('panel', 'group'))
The draws below stay inside these ranges and needn't reach their ends.
Inputs may be any that keep to these rules, and one draw needn't show every extreme that they name: `send_index`: each row is a permutation: every local node of a window is sent to exactly one slot. `support`: each row is a permutation: every received slot of a window is used by exactly one patch entry. `support_xyz`: each coordinate lies within 0.1 of its patch's centre. `panel_xyz`: each coordinate lies within 0.1 of its home patch's centre.
All inputs are finite; a program needn't handle non-finite values.
Results may differ from the reference program's by a relative error of at most 0.005.
Values may be sent and summed in bfloat16 or wider, within the bound.
No kernel may reach another device: no remote copies, remote signals or barrier semaphores. Data moves between devices by JAX's collectives and lax.ppermute only.
A program may use at most 192 MiB of HBM per device.

```python
import jax
import jax.numpy as jnp
from jax import lax

MODES = 32
SUPPORT = 64
PATCH_DEV = 256
PAN_DEV = 2048
SLOTS = 16384
NODE_DEV = 16384
PATCHES = 8192
PANELS = 65536
NODES = 524288
DEVICES = 32


def shared_layout(key):
    center_field = jax.random.uniform(jax.random.fold_in(key, 101), (3, PATCHES), jnp.float32, -1.0, 1.0)
    home_patch = jax.random.randint(jax.random.fold_in(key, 102), (PANELS,), 0, PATCH_DEV, dtype=jnp.int32)
    return (center_field, home_patch)


def draw_centers(key, part):
    center_field, home_patch = shared_layout(key)
    return center_field


def draw_member(key, part):
    center_field, home_patch = shared_layout(key)
    return home_patch


def draw_support_xyz(key, part):
    center_field, home_patch = shared_layout(key)
    key = jax.random.fold_in(key, 3)
    offset_field = jax.random.uniform(key, (3, PATCHES * SUPPORT), jnp.float32, -0.1, 0.1)
    return jnp.repeat(center_field, SUPPORT, axis=1) + offset_field


def draw_panel_xyz(key, part):
    center_field, home_patch = shared_layout(key)
    key = jax.random.fold_in(key, 4)
    window_of = jnp.arange(PANELS, dtype=jnp.int32) // PAN_DEV
    global_home = window_of * PATCH_DEV + home_patch
    base_field = jnp.take(center_field, global_home, axis=1)
    offset_field = jax.random.uniform(key, (3, PANELS), jnp.float32, -0.1, 0.1)
    return base_field + offset_field


def block_levels(stream_key, extent, cuts, smallest, top_value):
    gain, own = 1.0, jax.random.fold_in(stream_key, 6)
    for dim, blocks in cuts:
        heights = jnp.exp(jax.random.uniform(jax.random.fold_in(own, dim), (blocks,), jnp.float32, smallest / len(cuts), top_value / len(cuts)))
        gain = gain * jnp.repeat(heights, extent[dim] // blocks).reshape([-1 if axis == dim else 1 for axis in range(len(extent))])
    return gain


def centred(key, dims, spread, reach, cuts=(), held_as=jnp.bfloat16):
    loudness = block_levels(key, dims, cuts, -0.22, 0.18) if cuts else 1.0
    entries = jax.random.normal(key, dims, jnp.float32) * spread * loudness
    return jnp.minimum(jnp.maximum(entries, -reach), reach).astype(held_as)


def setup_inputs(seed: int = 0) -> dict:
    key_list = jax.random.split(jax.random.key(seed), 10)
    return {
        "displacement": centred(key_list[0], (3 * MODES, NODES), 1.0, 6.0, ((1, 32),)),
        "send_index": jax.vmap(lambda own: jax.random.permutation(own, NODE_DEV))(jax.random.split(key_list[1], DEVICES)).reshape((DEVICES, NODE_DEV)).astype(jnp.int32),
        "support": jax.vmap(lambda own: jax.random.permutation(own, SLOTS))(jax.random.split(key_list[2], DEVICES)).reshape((DEVICES, SLOTS)).astype(jnp.int32),
        "support_xyz": draw_support_xyz(jax.random.fold_in(key_list[9], 71), 0),
        "patch_kernel_inverse": centred(key_list[4], (SUPPORT, SUPPORT, PATCHES), SUPPORT ** -0.5, 0.75, ((0, 4), (2, 8))),
        "panel_xyz": draw_panel_xyz(jax.random.fold_in(key_list[9], 71), 0),
        "normals": centred(key_list[6], (3, PANELS), 0.6, 3.0, ((1, 32),), jnp.float32),
        "centers": draw_centers(jax.random.fold_in(key_list[9], 71), 0),
        "member": draw_member(jax.random.fold_in(key_list[9], 71), 0),
    }


KERNEL_RADIUS = 0.45
ATTRACTION_REACH = 0.3
OWNER_PREMIUM = 8.0

def compact_kernel(scaled):
    falloff = jnp.maximum(1.0 - scaled, 0.0)
    return falloff ** 4 * (4.0 * scaled + 1.0)

def blend_block(points, member, support_xyz, centers, support_count):
    dist_sq = (points[0][:, None] - support_xyz[0][None, :]) ** 2
    dist_sq = dist_sq + (points[1][:, None] - support_xyz[1][None, :]) ** 2
    dist_sq = dist_sq + (points[2][:, None] - support_xyz[2][None, :]) ** 2
    kernel = compact_kernel(jnp.sqrt(dist_sq) / KERNEL_RADIUS)
    center_distance_squared = (points[0][:, None] - centers[0][None, :]) ** 2
    center_distance_squared = center_distance_squared + (points[1][:, None] - centers[1][None, :]) ** 2
    center_distance_squared = center_distance_squared + (points[2][:, None] - centers[2][None, :]) ** 2
    patches = centers.shape[1]
    owner_patch = member[:, None] == jnp.arange(patches, dtype=jnp.int32)[None, :]
    patch_attraction = compact_kernel(jnp.sqrt(center_distance_squared) / ATTRACTION_REACH) + jnp.where(owner_patch, OWNER_PREMIUM, 0.0)
    weights = patch_attraction / lax.optimization_barrier(jnp.sum(patch_attraction, axis=1, keepdims=True))
    rows = points.shape[1]
    blended = kernel.reshape(rows, patches, support_count) * weights[:, :, None]
    return blended.reshape(rows, patches * support_count).astype(jnp.bfloat16)

def reference(displacement, send_index, support, support_xyz, patch_kernel_inverse, panel_xyz, normals, centers, member):
    per_peer = SLOTS // DEVICES
    send_table = send_index.reshape(DEVICES, DEVICES, per_peer)
    offsets = (jnp.arange(DEVICES, dtype=jnp.int32) * NODE_DEV)[:, None, None]
    node_ids = jnp.transpose(send_table + offsets, (1, 0, 2)).reshape(DEVICES, SLOTS)

    def window(window_index):
        received = jnp.take(displacement, node_ids[window_index], axis=1)
        values = jnp.take(received, support[window_index], axis=1).reshape(3 * MODES, PATCH_DEV, SUPPORT)
        inverse = lax.dynamic_slice_in_dim(patch_kernel_inverse, window_index * PATCH_DEV, PATCH_DEV, 2)
        coefficient = jnp.einsum('jkp,cpk->cpj', inverse.astype(jnp.float32), values.astype(jnp.float32)).astype(jnp.bfloat16)
        flat = coefficient.reshape(3 * MODES, SLOTS)
        points = lax.dynamic_slice_in_dim(panel_xyz, window_index * PAN_DEV, PAN_DEV, 1)
        facing = lax.dynamic_slice_in_dim(normals, window_index * PAN_DEV, PAN_DEV, 1)
        homes = lax.dynamic_slice_in_dim(member, window_index * PAN_DEV, PAN_DEV, 0)
        sources = lax.dynamic_slice_in_dim(support_xyz, window_index * SLOTS, SLOTS, 1)
        middles = lax.dynamic_slice_in_dim(centers, window_index * PATCH_DEV, PATCH_DEV, 1)
        blend = blend_block(points, homes, sources, middles, SUPPORT)
        moved = jnp.einsum('cs,ns->cn', flat.astype(jnp.float32), blend.astype(jnp.float32))
        moved = moved.reshape(3, MODES, PAN_DEV)
        return lax.optimization_barrier(jnp.sum(moved * facing[:, None, :], axis=0))
    result = lax.map(window, jnp.arange(DEVICES, dtype=jnp.int32))
    return jnp.transpose(result, (1, 0, 2)).reshape(MODES, PANELS)
```

```python
import functools

import jax
import jax.numpy as jnp
import numpy as np
from jax import lax
from jax.experimental import pallas as pl
from jax.experimental.pallas import tpu as pltpu
from jax.sharding import PartitionSpec as P

KERNEL_RADIUS = 0.45
ATTRACTION_REACH = 0.3
OWNER_PREMIUM = 8.0
LANES = 128
MIB = 1024 * 1024


def params(mib):
    return pltpu.CompilerParams(vmem_limit_bytes=mib * MIB)


def inverse_pack_kernel(inverse_ref, out_ref):
    half = inverse_ref.shape[0] // 2
    for a in range(half):
        pair = jnp.concatenate([inverse_ref[a], inverse_ref[a + half]], axis=0)
        turned = pair.astype(jnp.float32).T
        out_ref[0, :, a * LANES : (a + 1) * LANES] = turned.astype(jnp.bfloat16)


def inverse_pack(inverse, part, parts):
    rows, support_count, patches = inverse.shape
    windows = patches // (parts * LANES)
    return pl.pallas_call(
        inverse_pack_kernel,
        grid=(windows,),
        in_specs=[
            pl.BlockSpec((rows, support_count, LANES), lambda w: (0, 0, parts * w + part))
        ],
        out_specs=pl.BlockSpec((1, LANES, rows * support_count), lambda w: (w, 0, 0)),
        out_shape=jax.ShapeDtypeStruct((windows, LANES, rows * support_count), jnp.bfloat16),
        compiler_params=params(24),
        cost_estimate=pl.CostEstimate(
            flops=0, bytes_accessed=4 * inverse.size // parts, transcendentals=0
        ),
        name="inverse_pack",
    )(inverse)


def inverse_order(rows, support_count):
    half = rows // 2
    order = []
    for v in range(support_count // 16):
        for side in range(2):
            for i in range(8):
                r = 8 * v + i
                order.append((r // half) * rows + side * half + r % half)
    return np.array(order)


UNROLL = 32


def gather_rows(index_ref, source, target, base, count):
    def body(step, carry):
        for r in range(UNROLL):
            at = step * UNROLL + r
            target[pl.ds(at, 1), :] = source[pl.ds(index_ref[base + at], 1), :]
        return carry

    lax.fori_loop(0, count // UNROLL, body, 0)


def send_kernel(per, index_ref, displacement_ref, out_ref, rows_ref, block_ref):
    columns, nodes = displacement_ref.shape

    def turn(block, carry):
        at = pl.multiple_of(block * LANES, LANES)
        piece = displacement_ref[:, pl.ds(at, LANES)].astype(jnp.float32)
        piece = jnp.concatenate([piece, piece[: LANES - columns]], axis=0)
        rows_ref[pl.ds(at, LANES), :] = piece.T
        return carry

    lax.fori_loop(0, nodes // LANES, turn, 0)
    quarter = per // 4
    lane = lax.broadcasted_iota(jnp.int32, (quarter, LANES), 1)

    def peer(d, carry):
        gather_rows(index_ref, rows_ref, block_ref, d * per, per)
        last = block_ref[3 * quarter : 4 * quarter, :]
        for i in range(3):
            own = block_ref[i * quarter : (i + 1) * quarter, :]
            full = jnp.where(lane < 96, own, pltpu.roll(last, 96 - 32 * i, 1))
            at = pl.multiple_of(d * 3 * quarter + i * quarter, quarter)
            out_ref[pl.ds(at, quarter), :] = full.astype(jnp.bfloat16)
        return carry

    lax.fori_loop(0, nodes // per, peer, 0)


def send_rows(displacement, index, per):
    columns, nodes = displacement.shape
    return pl.pallas_call(
        functools.partial(send_kernel, per),
        in_specs=[
            pl.BlockSpec(memory_space=pltpu.SMEM),
            pl.BlockSpec(memory_space=pltpu.VMEM),
        ],
        out_specs=pl.BlockSpec(memory_space=pltpu.VMEM),
        out_shape=jax.ShapeDtypeStruct((nodes * 3 // 4, LANES), jnp.bfloat16),
        scratch_shapes=[
            pltpu.VMEM((nodes, LANES), jnp.float32),
            pltpu.VMEM((per, LANES), jnp.float32),
        ],
        compiler_params=params(32),
        cost_estimate=pl.CostEstimate(
            flops=0, bytes_accessed=60 * MIB, transcendentals=0
        ),
        name="send_rows",
    )(index, displacement)


def receive_kernel(per, index_ref, packed_ref, out_ref, rows_ref, block_ref):
    slots = rows_ref.shape[0]
    quarter = per // 4
    lane = lax.broadcasted_iota(jnp.int32, (quarter, LANES), 1)

    def peer(d, carry):
        parts = []
        for i in range(3):
            at = pl.multiple_of(d * 3 * quarter + i * quarter, quarter)
            piece = packed_ref[pl.ds(at, quarter), :].astype(jnp.float32)
            parts.append(pltpu.roll(piece, 32 * (i + 1), 1))
            to = pl.multiple_of(d * per + i * quarter, quarter)
            rows_ref[pl.ds(to, quarter), :] = piece
        last = jnp.where(lane < 32, parts[0], jnp.where(lane < 64, parts[1], parts[2]))
        to = pl.multiple_of(d * per + 3 * quarter, quarter)
        rows_ref[pl.ds(to, quarter), :] = last
        return carry

    lax.fori_loop(0, slots // per, peer, 0)
    chunk = block_ref.shape[0]

    def pick(b, carry):
        gather_rows(index_ref, rows_ref, block_ref, b * chunk, chunk)
        at = pl.multiple_of(b * chunk, chunk)
        out_ref[pl.ds(at, chunk), :] = block_ref[...].astype(jnp.bfloat16)
        return carry

    lax.fori_loop(0, slots // chunk, pick, 0)


def receive_rows(packed, index, per):
    slots = index.shape[0]
    return pl.pallas_call(
        functools.partial(receive_kernel, per),
        in_specs=[
            pl.BlockSpec(memory_space=pltpu.SMEM),
            pl.BlockSpec(memory_space=pltpu.VMEM),
        ],
        out_specs=pl.BlockSpec(memory_space=pltpu.VMEM),
        out_shape=jax.ShapeDtypeStruct((slots, LANES), jnp.bfloat16),
        scratch_shapes=[
            pltpu.VMEM((slots, LANES), jnp.float32),
            pltpu.VMEM((256, LANES), jnp.float32),
        ],
        compiler_params=params(32),
        cost_estimate=pl.CostEstimate(
            flops=0, bytes_accessed=60 * MIB, transcendentals=0
        ),
        name="receive_rows",
    )(index, packed)


def splits(x):
    high = x.astype(jnp.bfloat16).astype(jnp.float32)
    rest = x - high
    middle = rest.astype(jnp.bfloat16).astype(jnp.float32)
    return high, middle, rest - middle


def distance_rows(xyz, entry_side):
    rows = []
    square = None
    for c in range(3):
        x = xyz[c : c + 1, :] * (1.0 / KERNEL_RADIUS)
        square = x * x if square is None else square + x * x
        if entry_side:
            s1, s2, s3 = splits(-2.0 * x)
            rows += [s1, s1, s2, s2, s1, s3]
        else:
            p1, p2, p3 = splits(x)
            rows += [p1, p2, p1, p2, p3, p1]
    one = jnp.ones_like(square)
    own = list(splits(square))
    rows += own + [one] * 3 if entry_side else [one] * 3 + own
    rows += [jnp.zeros_like(square)] * 8
    return jnp.concatenate(rows, axis=0)


def falloff_terms(scaled_sq):
    safe = jnp.maximum(scaled_sq, 1e-12)
    return jnp.maximum(1.0 - safe * lax.rsqrt(safe), 0.0)


PANEL_CHUNK = 256


def blend_kernel(
    support_count,
    points_ref,
    member_ref,
    centers_ref,
    support_ref,
    out_ref,
    panel_rows,
    five_ref,
    four_ref,
):
    panels = points_ref.shape[1]
    patches = centers_ref.shape[0]
    entries = support_ref.shape[1]
    block_patches = entries // support_count
    step = pl.program_id(0)

    @pl.when(step == 0)
    def _():
        panel_rows[...] = distance_rows(points_ref[...], False).astype(jnp.bfloat16)
        patch = lax.broadcasted_iota(jnp.int32, (patches, LANES), 0)

        def weigh(b, carry):
            at = pl.multiple_of(b * LANES, LANES)
            square = None
            for c in range(3):
                gap = centers_ref[:, c : c + 1] - points_ref[c : c + 1, pl.ds(at, LANES)]
                square = gap * gap if square is None else square + gap * gap
            u = falloff_terms(square * (1.0 / ATTRACTION_REACH**2))
            u2 = u * u
            owner = jnp.where(member_ref[:, pl.ds(at, LANES)] == patch, OWNER_PREMIUM, 0.0)
            attraction = u2 * u2 * (5.0 - 4.0 * u) + owner
            weight = attraction / jnp.sum(attraction, axis=0, keepdims=True)
            five_ref[:, pl.ds(at, LANES)] = 5.0 * weight
            four_ref[:, pl.ds(at, LANES)] = 4.0 * weight
            return carry

        lax.fori_loop(0, panels // LANES, weigh, 0)

    entry_rows = distance_rows(support_ref[...], True).T.astype(jnp.bfloat16)

    def chunk(b, carry):
        at = pl.multiple_of(b * PANEL_CHUNK, PANEL_CHUNK)
        first = pl.multiple_of(step * block_patches, block_patches)
        five = five_ref[pl.ds(first, block_patches), pl.ds(at, PANEL_CHUNK)]
        four = four_ref[pl.ds(first, block_patches), pl.ds(at, PANEL_CHUNK)]
        columns = panel_rows[:, pl.ds(at, PANEL_CHUNK)]
        for p in range(block_patches):
            rows = slice(p * support_count, (p + 1) * support_count)
            square = jnp.dot(entry_rows[rows], columns, preferred_element_type=jnp.float32)
            u = falloff_terms(square)
            u2 = u * u
            value = u2 * u2 * (five[p : p + 1] - four[p : p + 1] * u)
            out_ref[rows, pl.ds(at, PANEL_CHUNK)] = value.astype(jnp.bfloat16)
        return carry

    lax.fori_loop(0, panels // PANEL_CHUNK, chunk, 0)


def blend_entry_major(points, member, support_xyz, centers, support_count):
    panels = points.shape[1]
    patches = centers.shape[1]
    slots = support_xyz.shape[1]
    block = 8 * support_count
    return pl.pallas_call(
        functools.partial(blend_kernel, support_count),
        grid=(slots // block,),
        in_specs=[
            pl.BlockSpec((3, panels), lambda i: (0, 0)),
            pl.BlockSpec((1, panels), lambda i: (0, 0)),
            pl.BlockSpec((patches, 3), lambda i: (0, 0)),
            pl.BlockSpec((3, block), lambda i: (0, i)),
        ],
        out_specs=pl.BlockSpec((block, panels), lambda i: (i, 0)),
        out_shape=jax.ShapeDtypeStruct((slots, panels), jnp.bfloat16),
        scratch_shapes=[
            pltpu.VMEM((32, panels), jnp.bfloat16),
            pltpu.VMEM((patches, panels), jnp.float32),
            pltpu.VMEM((patches, panels), jnp.float32),
        ],
        compiler_params=params(40),
        cost_estimate=pl.CostEstimate(
            flops=64 * slots * panels,
            bytes_accessed=4 * slots * panels,
            transcendentals=slots * panels,
        ),
        name="blend",
    )(points, member.reshape(1, panels), centers.T, support_xyz)


def moved_kernel(modes, last, support_count, *refs):
    if last:
        inverse_ref, values_ref, blend_ref, start_ref, normals_ref, out_ref = refs[:6]
        turned_ref, total_ref, coef_ref = refs[6:]
    else:
        inverse_ref, values_ref, blend_ref, out_ref = refs[:4]
        turned_ref, coef_ref = refs[4:]
        total_ref = out_ref
    step = pl.program_id(0)

    @pl.when(step == 0)
    def _():
        if last:
            total_ref[...] = start_ref[...]
        else:
            total_ref[...] = jnp.zeros_like(total_ref)

    owners, block_patches, width = inverse_ref.shape
    halves = width // LANES
    per_patch = owners * halves
    for o in range(owners):
        for a in range(halves):
            piece = inverse_ref[o, :, a * LANES : (a + 1) * LANES].astype(jnp.float32)
            turned_ref[pl.ds(o * halves + a, block_patches, stride=per_patch), :] = piece
    lane = lax.broadcasted_iota(jnp.int32, (8, LANES), 1)
    low = lane < support_count
    for pair in range(block_patches // 2):
        rows = []
        for side in range(2):
            for v in range(per_patch // 8):
                at = (2 * pair + side) * per_patch + 8 * v
                own = turned_ref[at : at + 8, :]
                other = pltpu.roll(own, support_count, 1)
                both = (own, other) if side == 0 else (other, own)
                keep = low if side == 0 else jnp.logical_not(low)
                rows += [jnp.where(keep, x, 0.0) for x in both]
        block = jnp.concatenate(rows, axis=0).astype(jnp.bfloat16)
        at = pair * LANES
        coef = jnp.dot(
            block, values_ref[at : at + LANES, :], preferred_element_type=jnp.float32
        )
        coef_ref[:, at : at + LANES] = coef.T[: 3 * modes].astype(jnp.bfloat16)
    total_ref[...] += jnp.dot(
        coef_ref[...], blend_ref[...], preferred_element_type=jnp.float32
    )

    if last:

        @pl.when(step == pl.num_programs(0) - 1)
        def _():
            result = None
            for c in range(3):
                term = normals_ref[c : c + 1, :] * total_ref[c * modes : (c + 1) * modes, :]
                result = term if result is None else result + term
            out_ref[...] = result


def moved_part(inverse, values, blend, part, modes, support_count, start=None, normals=None):
    owners, patches, width = inverse.shape
    slots, panels = blend.shape
    block_patches = 16
    steps = patches // block_patches
    block = block_patches * support_count
    last = start is not None
    in_specs = [
        pl.BlockSpec((owners, block_patches, width), lambda i: (0, i, 0)),
        pl.BlockSpec((block, LANES), lambda i: (part * steps + i, 0)),
        pl.BlockSpec((block, panels), lambda i: (part * steps + i, 0)),
    ]
    operands = [inverse, values, blend]
    total_shape = (3 * modes, panels)
    scratch = [pltpu.VMEM((block_patches * support_count // 2, LANES), jnp.float32)]
    if last:
        in_specs += [
            pl.BlockSpec(total_shape, lambda i: (0, 0)),
            pl.BlockSpec((3, panels), lambda i: (0, 0)),
        ]
        operands += [start, normals]
        scratch += [pltpu.VMEM(total_shape, jnp.float32)]
        out_shape = (modes, panels)
    else:
        out_shape = total_shape
    scratch += [pltpu.VMEM((3 * modes, block), jnp.bfloat16)]
    return pl.pallas_call(
        functools.partial(moved_kernel, modes, last, support_count),
        grid=(steps,),
        in_specs=in_specs,
        out_specs=pl.BlockSpec(out_shape, lambda i: (0, 0)),
        out_shape=jax.ShapeDtypeStruct(out_shape, jnp.float32),
        scratch_shapes=scratch,
        compiler_params=params(40),
        cost_estimate=pl.CostEstimate(
            flops=2 * 3 * modes * panels * patches * support_count,
            bytes_accessed=2 * panels * patches * support_count,
            transcendentals=0,
        ),
        name="moved_last" if last else "moved_first",
    )(*operands)


def shards(

    displacement,
    send_index,
    support,
    support_xyz,
    patch_kernel_inverse,
    panel_xyz,
    normals,
    centers,
    member,
):
    axes = ("panel", "group")
    columns = displacement.shape[0]
    modes = columns // 3
    slots = send_index.shape[1]
    patches = centers.shape[1]
    support_count = slots // patches
    devices = lax.axis_size(axes)
    per = slots // devices
    parts = patches // LANES

    own_rows = patch_kernel_inverse.shape[0]
    order = inverse_order(own_rows, support_count)
    if not np.array_equal(order, np.arange(support_count)):
        xyz = support_xyz.reshape(3, patches, support_count)
        support_xyz = jnp.take(xyz, order, axis=2).reshape(3, slots)

    def exchange(packed):
        got = lax.all_to_all(packed, "group", split_axis=0, concat_axis=0, tiled=True)
        return got

    first = exchange(inverse_pack(patch_kernel_inverse, 0, parts))
    second_packed = inverse_pack(patch_kernel_inverse, 1, parts)
    outgoing = send_rows(displacement, send_index.reshape(slots), per)
    arriving = lax.all_to_all(
        outgoing.reshape(devices, per * 3 // 4, LANES), axes, 0, 0, tiled=True
    ).reshape(slots * 3 // 4, LANES)
    second_packed, _ = lax.optimization_barrier((second_packed, outgoing))
    second = exchange(second_packed)
    blend = blend_entry_major(panel_xyz, member, support_xyz, centers, support_count)
    values = receive_rows(arriving, support.reshape(slots), per)
    total = moved_part(first, values, blend, 0, modes, support_count)
    return moved_part(second, values, blend, 1, modes, support_count, total, normals)


def solution(mesh):
    return jax.shard_map(
        shards,
        mesh=mesh,
        in_specs=(
            P(None, ("panel", "group")),
            P(("panel", "group"), None),
            P(("panel", "group"), None),
            P(None, ("panel", "group")),
            P("group", None, "panel"),
            P(None, ("panel", "group")),
            P(None, ("panel", "group")),
            P(None, ("panel", "group")),
            P(("panel", "group")),
        ),
        out_specs=P(None, ("panel", "group")),
        check_vma=False,
    )
```

```python
import functools

import jax
import jax.numpy as jnp
import numpy as np
from jax import lax
from jax.experimental import pallas as pl
from jax.experimental.pallas import tpu as pltpu
from jax.sharding import PartitionSpec as P

KERNEL_RADIUS = 0.45
ATTRACTION_REACH = 0.3
OWNER_PREMIUM = 8.0
LANES = 128
MIB = 1024 * 1024


def params(mib):
    return pltpu.CompilerParams(vmem_limit_bytes=mib * MIB)


def inverse_pack_kernel(inverse_ref, out_ref):
    half = inverse_ref.shape[0] // 2
    for a in range(half):
        pair = jnp.concatenate([inverse_ref[a], inverse_ref[a + half]], axis=0)
        turned = pair.astype(jnp.float32).T
        out_ref[0, :, a * LANES : (a + 1) * LANES] = turned.astype(jnp.bfloat16)


def inverse_pack(inverse, part, parts):
    rows, support_count, patches = inverse.shape
    windows = patches // (parts * LANES)
    return pl.pallas_call(
        inverse_pack_kernel,
        grid=(windows,),
        in_specs=[
            pl.BlockSpec((rows, support_count, LANES), lambda w: (0, 0, parts * w + part))
        ],
        out_specs=pl.BlockSpec((1, LANES, rows * support_count), lambda w: (w, 0, 0)),
        out_shape=jax.ShapeDtypeStruct((windows, LANES, rows * support_count), jnp.bfloat16),
        compiler_params=params(24),
        cost_estimate=pl.CostEstimate(
            flops=0, bytes_accessed=4 * inverse.size // parts, transcendentals=0
        ),
        name="inverse_pack",
    )(inverse)


def inverse_order(rows, support_count):
    half = rows // 2
    order = []
    for v in range(support_count // 16):
        for side in range(2):
            for i in range(8):
                r = 8 * v + i
                order.append((r // half) * rows + side * half + r % half)
    return np.array(order)


UNROLL = 32


def gather_rows(index_ref, source, target, base, count):
    def body(step, carry):
        for r in range(UNROLL):
            at = step * UNROLL + r
            target[pl.ds(at, 1), :] = source[pl.ds(index_ref[base + at], 1), :]
        return carry

    lax.fori_loop(0, count // UNROLL, body, 0)


def send_kernel(per, index_ref, displacement_ref, out_ref, rows_ref, block_ref):
    columns, nodes = displacement_ref.shape

    def turn(block, carry):
        at = pl.multiple_of(block * LANES, LANES)
        piece = displacement_ref[:, pl.ds(at, LANES)].astype(jnp.float32)
        piece = jnp.concatenate([piece, piece[: LANES - columns]], axis=0)
        rows_ref[pl.ds(at, LANES), :] = piece.T
        return carry

    lax.fori_loop(0, nodes // LANES, turn, 0)
    quarter = per // 4
    lane = lax.broadcasted_iota(jnp.int32, (quarter, LANES), 1)

    def peer(d, carry):
        gather_rows(index_ref, rows_ref, block_ref, d * per, per)
        last = block_ref[3 * quarter : 4 * quarter, :]
        for i in range(3):
            own = block_ref[i * quarter : (i + 1) * quarter, :]
            full = jnp.where(lane < 96, own, pltpu.roll(last, 96 - 32 * i, 1))
            at = pl.multiple_of(d * 3 * quarter + i * quarter, quarter)
            out_ref[pl.ds(at, quarter), :] = full.astype(jnp.bfloat16)
        return carry

    lax.fori_loop(0, nodes // per, peer, 0)


def send_rows(displacement, index, per):
    columns, nodes = displacement.shape
    return pl.pallas_call(
        functools.partial(send_kernel, per),
        in_specs=[
            pl.BlockSpec(memory_space=pltpu.SMEM),
            pl.BlockSpec(memory_space=pltpu.VMEM),
        ],
        out_specs=pl.BlockSpec(memory_space=pltpu.VMEM),
        out_shape=jax.ShapeDtypeStruct((nodes * 3 // 4, LANES), jnp.bfloat16),
        scratch_shapes=[
            pltpu.VMEM((nodes, LANES), jnp.float32),
            pltpu.VMEM((per, LANES), jnp.float32),
        ],
        compiler_params=params(32),
        cost_estimate=pl.CostEstimate(
            flops=0, bytes_accessed=60 * MIB, transcendentals=0
        ),
        name="send_rows",
    )(index, displacement)


def receive_kernel(per, index_ref, packed_ref, out_ref, rows_ref, block_ref):
    slots = rows_ref.shape[0]
    quarter = per // 4
    lane = lax.broadcasted_iota(jnp.int32, (quarter, LANES), 1)

    def peer(d, carry):
        parts = []
        for i in range(3):
            at = pl.multiple_of(d * 3 * quarter + i * quarter, quarter)
            piece = packed_ref[pl.ds(at, quarter), :].astype(jnp.float32)
            parts.append(pltpu.roll(piece, 32 * (i + 1), 1))
            to = pl.multiple_of(d * per + i * quarter, quarter)
            rows_ref[pl.ds(to, quarter), :] = piece
        last = jnp.where(lane < 32, parts[0], jnp.where(lane < 64, parts[1], parts[2]))
        to = pl.multiple_of(d * per + 3 * quarter, quarter)
        rows_ref[pl.ds(to, quarter), :] = last
        return carry

    lax.fori_loop(0, slots // per, peer, 0)
    chunk = block_ref.shape[0]

    def pick(b, carry):
        gather_rows(index_ref, rows_ref, block_ref, b * chunk, chunk)
        at = pl.multiple_of(b * chunk, chunk)
        out_ref[pl.ds(at, chunk), :] = block_ref[...].astype(jnp.bfloat16)
        return carry

    lax.fori_loop(0, slots // chunk, pick, 0)


def receive_rows(packed, index, per):
    slots = index.shape[0]
    return pl.pallas_call(
        functools.partial(receive_kernel, per),
        in_specs=[
            pl.BlockSpec(memory_space=pltpu.SMEM),
            pl.BlockSpec(memory_space=pltpu.VMEM),
        ],
        out_specs=pl.BlockSpec(memory_space=pltpu.VMEM),
        out_shape=jax.ShapeDtypeStruct((slots, LANES), jnp.bfloat16),
        scratch_shapes=[
            pltpu.VMEM((slots, LANES), jnp.float32),
            pltpu.VMEM((256, LANES), jnp.float32),
        ],
        compiler_params=params(32),
        cost_estimate=pl.CostEstimate(
            flops=0, bytes_accessed=60 * MIB, transcendentals=0
        ),
        name="receive_rows",
    )(index, packed)


def splits(x):
    high = x.astype(jnp.bfloat16).astype(jnp.float32)
    rest = x - high
    middle = rest.astype(jnp.bfloat16).astype(jnp.float32)
    return high, middle, rest - middle


def distance_rows(xyz, entry_side):
    rows = []
    square = None
    for c in range(3):
        x = xyz[c : c + 1, :] * (1.0 / KERNEL_RADIUS)
        square = x * x if square is None else square + x * x
        if entry_side:
            s1, s2, s3 = splits(-2.0 * x)
            rows += [s1, s1, s2, s2, s1, s3]
        else:
            p1, p2, p3 = splits(x)
            rows += [p1, p2, p1, p2, p3, p1]
    one = jnp.ones_like(square)
    own = list(splits(square))
    rows += own + [one] * 3 if entry_side else [one] * 3 + own
    rows += [jnp.zeros_like(square)] * 8
    return jnp.concatenate(rows, axis=0)


def falloff_terms(scaled_sq):
    safe = jnp.maximum(scaled_sq, 1e-12)
    return jnp.maximum(1.0 - safe * lax.rsqrt(safe), 0.0)


PANEL_CHUNK = 256


def blend_kernel(
    support_count,
    points_ref,
    member_ref,
    centers_ref,
    support_ref,
    out_ref,
    panel_rows,
    five_ref,
    four_ref,
):
    panels = points_ref.shape[1]
    patches = centers_ref.shape[0]
    entries = support_ref.shape[1]
    block_patches = entries // support_count
    step = pl.program_id(0)

    @pl.when(step == 0)
    def _():
        panel_rows[...] = distance_rows(points_ref[...], False).astype(jnp.bfloat16)
        patch = lax.broadcasted_iota(jnp.int32, (patches, LANES), 0)

        def weigh(b, carry):
            at = pl.multiple_of(b * LANES, LANES)
            square = None
            for c in range(3):
                gap = centers_ref[:, c : c + 1] - points_ref[c : c + 1, pl.ds(at, LANES)]
                square = gap * gap if square is None else square + gap * gap
            u = falloff_terms(square * (1.0 / ATTRACTION_REACH**2))
            u2 = u * u
            owner = jnp.where(member_ref[:, pl.ds(at, LANES)] == patch, OWNER_PREMIUM, 0.0)
            attraction = u2 * u2 * (5.0 - 4.0 * u) + owner
            weight = attraction / jnp.sum(attraction, axis=0, keepdims=True)
            five_ref[:, pl.ds(at, LANES)] = 5.0 * weight
            four_ref[:, pl.ds(at, LANES)] = 4.0 * weight
            return carry

        lax.fori_loop(0, panels // LANES, weigh, 0)

    entry_rows = distance_rows(support_ref[...], True).T.astype(jnp.bfloat16)

    def chunk(b, carry):
        at = pl.multiple_of(b * PANEL_CHUNK, PANEL_CHUNK)
        first = pl.multiple_of(step * block_patches, block_patches)
        five = five_ref[pl.ds(first, block_patches), pl.ds(at, PANEL_CHUNK)]
        four = four_ref[pl.ds(first, block_patches), pl.ds(at, PANEL_CHUNK)]
        columns = panel_rows[:, pl.ds(at, PANEL_CHUNK)]
        for p in range(block_patches):
            rows = slice(p * support_count, (p + 1) * support_count)
            square = jnp.dot(entry_rows[rows], columns, preferred_element_type=jnp.float32)
            u = falloff_terms(square)
            u2 = u * u
            value = u2 * u2 * (five[p : p + 1] - four[p : p + 1] * u)
            out_ref[rows, pl.ds(at, PANEL_CHUNK)] = value.astype(jnp.bfloat16)
        return carry

    lax.fori_loop(0, panels // PANEL_CHUNK, chunk, 0)


def blend_entry_major(points, member, support_xyz, centers, support_count):
    panels = points.shape[1]
    patches = centers.shape[1]
    slots = support_xyz.shape[1]
    block = 8 * support_count
    return pl.pallas_call(
        functools.partial(blend_kernel, support_count),
        grid=(slots // block,),
        in_specs=[
            pl.BlockSpec((3, panels), lambda i: (0, 0)),
            pl.BlockSpec((1, panels), lambda i: (0, 0)),
            pl.BlockSpec((patches, 3), lambda i: (0, 0)),
            pl.BlockSpec((3, block), lambda i: (0, i)),
        ],
        out_specs=pl.BlockSpec((block, panels), lambda i: (i, 0)),
        out_shape=jax.ShapeDtypeStruct((slots, panels), jnp.bfloat16),
        scratch_shapes=[
            pltpu.VMEM((32, panels), jnp.bfloat16),
            pltpu.VMEM((patches, panels), jnp.float32),
            pltpu.VMEM((patches, panels), jnp.float32),
        ],
        compiler_params=params(40),
        cost_estimate=pl.CostEstimate(
            flops=64 * slots * panels,
            bytes_accessed=4 * slots * panels,
            transcendentals=slots * panels,
        ),
        name="blend",
    )(points, member.reshape(1, panels), centers.T, support_xyz)


def moved_kernel(modes, last, support_count, *refs):
    if last:
        inverse_ref, values_ref, blend_ref, start_ref, normals_ref, out_ref = refs[:6]
        turned_ref, total_ref, coef_ref = refs[6:]
    else:
        inverse_ref, values_ref, blend_ref, out_ref = refs[:4]
        turned_ref, coef_ref = refs[4:]
        total_ref = out_ref
    step = pl.program_id(0)

    @pl.when(step == 0)
    def _():
        if last:
            total_ref[...] = start_ref[...]
        else:
            total_ref[...] = jnp.zeros_like(total_ref)

    owners, block_patches, width = inverse_ref.shape
    halves = width // LANES
    per_patch = owners * halves
    for o in range(owners):
        for a in range(halves):
            piece = inverse_ref[o, :, a * LANES : (a + 1) * LANES].astype(jnp.float32)
            turned_ref[pl.ds(o * halves + a, block_patches, stride=per_patch), :] = piece
    lane = lax.broadcasted_iota(jnp.int32, (8, LANES), 1)
    low = lane < support_count
    for pair in range(block_patches // 2):
        rows = []
        for side in range(2):
            for v in range(per_patch // 8):
                at = (2 * pair + side) * per_patch + 8 * v
                own = turned_ref[at : at + 8, :]
                other = pltpu.roll(own, support_count, 1)
                both = (own, other) if side == 0 else (other, own)
                keep = low if side == 0 else jnp.logical_not(low)
                rows += [jnp.where(keep, x, 0.0) for x in both]
        block = jnp.concatenate(rows, axis=0).astype(jnp.bfloat16)
        at = pair * LANES
        coef = jnp.dot(
            block, values_ref[at : at + LANES, :], preferred_element_type=jnp.float32
        )
        coef_ref[:, at : at + LANES] = coef.T[: 3 * modes].astype(jnp.bfloat16)
    total_ref[...] += jnp.dot(
        coef_ref[...], blend_ref[...], preferred_element_type=jnp.float32
    )

    if last:

        @pl.when(step == pl.num_programs(0) - 1)
        def _():
            result = None
            for c in range(3):
                term = normals_ref[c : c + 1, :] * total_ref[c * modes : (c + 1) * modes, :]
                result = term if result is None else result + term
            out_ref[...] = result


def moved_part(inverse, values, blend, part, modes, support_count, start=None, normals=None):
    owners, patches, width = inverse.shape
    slots, panels = blend.shape
    block_patches = 16
    steps = patches // block_patches
    block = block_patches * support_count
    last = start is not None
    in_specs = [
        pl.BlockSpec((owners, block_patches, width), lambda i: (0, i, 0)),
        pl.BlockSpec((block, LANES), lambda i: (part * steps + i, 0)),
        pl.BlockSpec((block, panels), lambda i: (part * steps + i, 0)),
    ]
    operands = [inverse, values, blend]
    total_shape = (3 * modes, panels)
    scratch = [pltpu.VMEM((block_patches * support_count // 2, LANES), jnp.float32)]
    if last:
        in_specs += [
            pl.BlockSpec(total_shape, lambda i: (0, 0)),
            pl.BlockSpec((3, panels), lambda i: (0, 0)),
        ]
        operands += [start, normals]
        scratch += [pltpu.VMEM(total_shape, jnp.float32)]
        out_shape = (modes, panels)
    else:
        out_shape = total_shape
    scratch += [pltpu.VMEM((3 * modes, block), jnp.bfloat16)]
    return pl.pallas_call(
        functools.partial(moved_kernel, modes, last, support_count),
        grid=(steps,),
        in_specs=in_specs,
        out_specs=pl.BlockSpec(out_shape, lambda i: (0, 0)),
        out_shape=jax.ShapeDtypeStruct(out_shape, jnp.float32),
        scratch_shapes=scratch,
        compiler_params=params(40),
        cost_estimate=pl.CostEstimate(
            flops=2 * 3 * modes * panels * patches * support_count,
            bytes_accessed=2 * panels * patches * support_count,
            transcendentals=0,
        ),
        name="moved_last" if last else "moved_first",
    )(*operands)


def shards(

    displacement,
    send_index,
    support,
    support_xyz,
    patch_kernel_inverse,
    panel_xyz,
    normals,
    centers,
    member,
):
    axes = ("panel", "group")
    columns = displacement.shape[0]
    modes = columns // 3
    slots = send_index.shape[1]
    patches = centers.shape[1]
    support_count = slots // patches
    devices = lax.axis_size(axes)
    per = slots // devices
    parts = patches // LANES

    own_rows = patch_kernel_inverse.shape[0]
    order = inverse_order(own_rows, support_count)
    if not np.array_equal(order, np.arange(support_count)):
        xyz = support_xyz.reshape(3, patches, support_count)
        support_xyz = jnp.take(xyz, order, axis=2).reshape(3, slots)

    def exchange(packed):
        got = lax.all_to_all(packed, "group", split_axis=0, concat_axis=0, tiled=True)
        return got

    first = exchange(inverse_pack(patch_kernel_inverse, 0, parts))
    second_packed = inverse_pack(patch_kernel_inverse, 1, parts)
    outgoing = send_rows(displacement, send_index.reshape(slots), per)
    outgoing, panel_xyz = lax.optimization_barrier((outgoing, panel_xyz))
    arriving = lax.all_to_all(
        outgoing.reshape(devices, per * 3 // 4, LANES), axes, 0, 0, tiled=True
    ).reshape(slots * 3 // 4, LANES)
    blend = blend_entry_major(panel_xyz, member, support_xyz, centers, support_count)
    blend, second_packed, support = lax.optimization_barrier((blend, second_packed, support))
    second = exchange(second_packed)
    values = receive_rows(arriving, support.reshape(slots), per)
    total = moved_part(first, values, blend, 0, modes, support_count)
    return moved_part(second, values, blend, 1, modes, support_count, total, normals)


def solution(mesh):
    return jax.shard_map(
        shards,
        mesh=mesh,
        in_specs=(
            P(None, ("panel", "group")),
            P(("panel", "group"), None),
            P(("panel", "group"), None),
            P(None, ("panel", "group")),
            P("group", None, "panel"),
            P(None, ("panel", "group")),
            P(None, ("panel", "group")),
            P(None, ("panel", "group")),
            P(("panel", "group")),
        ),
        out_specs=P(None, ("panel", "group")),
        check_vma=False,
    )
```

```python
import functools

import jax
import jax.numpy as jnp
import numpy as np
from jax import lax
from jax.experimental import pallas as pl
from jax.experimental.pallas import tpu as pltpu
from jax.sharding import PartitionSpec as P

KERNEL_RADIUS = 0.45
ATTRACTION_REACH = 0.3
OWNER_PREMIUM = 8.0
LANES = 128
MIB = 1024 * 1024


def params(mib):
    return pltpu.CompilerParams(vmem_limit_bytes=mib * MIB)


def inverse_pack_kernel(window_ref, inverse_ref, out_ref):
    half = inverse_ref.shape[0] // 2
    for a in range(half):
        pair = jnp.concatenate([inverse_ref[a], inverse_ref[a + half]], axis=0)
        turned = pair.astype(jnp.float32).T
        out_ref[:, a * LANES : (a + 1) * LANES] = turned.astype(jnp.bfloat16)


def inverse_pack(inverse, window, patches):
    rows, support_count, _ = inverse.shape
    parts = patches // LANES
    width = rows * support_count
    return pl.pallas_call(
        inverse_pack_kernel,
        grid_spec=pltpu.PrefetchScalarGridSpec(
            num_scalar_prefetch=1,
            grid=(parts,),
            in_specs=[
                pl.BlockSpec(
                    (rows, support_count, LANES), lambda i, w: (0, 0, parts * w[0] + i)
                )
            ],
            out_specs=pl.BlockSpec((LANES, width), lambda i, w: (i, 0)),
        ),
        out_shape=jax.ShapeDtypeStruct((patches, width), jnp.bfloat16),
        compiler_params=params(24),
        cost_estimate=pl.CostEstimate(
            flops=0, bytes_accessed=4 * patches * width, transcendentals=0
        ),
        name="inverse_pack",
    )(window.reshape(1), inverse)


def inverse_order(rows, support_count):
    half = rows // 2
    order = []
    for v in range(support_count // 16):
        for side in range(2):
            for i in range(8):
                r = 8 * v + i
                order.append((r // half) * rows + side * half + r % half)
    return np.array(order)


UNROLL = 128


def gather_rows(index_ref, source, target, base, count):
    def body(step, carry):
        for r in range(UNROLL):
            at = step * UNROLL + r
            target[pl.ds(at, 1), :] = source[pl.ds(index_ref[base + at], 1), :]
        return carry

    lax.fori_loop(0, count // UNROLL, body, 0)


def send_kernel(per, index_ref, displacement_ref, out_ref, rows_ref, block_ref):
    columns, nodes = displacement_ref.shape

    def turn(block, carry):
        at = pl.multiple_of(block * LANES, LANES)
        piece = displacement_ref[:, pl.ds(at, LANES)].astype(jnp.float32)
        piece = jnp.concatenate([piece, piece[: LANES - columns]], axis=0)
        rows_ref[pl.ds(at, LANES), :] = piece.T
        return carry

    lax.fori_loop(0, nodes // LANES, turn, 0, unroll=4)
    quarter = per // 4
    lane = lax.broadcasted_iota(jnp.int32, (quarter, LANES), 1)

    def peer(d, carry):
        gather_rows(index_ref, rows_ref, block_ref, d * per, per)
        last = block_ref[3 * quarter : 4 * quarter, :]
        for i in range(3):
            own = block_ref[i * quarter : (i + 1) * quarter, :]
            full = jnp.where(lane < 96, own, pltpu.roll(last, 96 - 32 * i, 1))
            at = pl.multiple_of(d * 3 * quarter + i * quarter, quarter)
            out_ref[pl.ds(at, quarter), :] = full.astype(jnp.bfloat16)
        return carry

    lax.fori_loop(0, nodes // per, peer, 0)


def send_rows(displacement, index, per):
    columns, nodes = displacement.shape
    return pl.pallas_call(
        functools.partial(send_kernel, per),
        in_specs=[
            pl.BlockSpec(memory_space=pltpu.SMEM),
            pl.BlockSpec(memory_space=pltpu.VMEM),
        ],
        out_specs=pl.BlockSpec(memory_space=pltpu.VMEM),
        out_shape=jax.ShapeDtypeStruct((nodes * 3 // 4, LANES), jnp.bfloat16),
        scratch_shapes=[
            pltpu.VMEM((nodes, LANES), jnp.float32),
            pltpu.VMEM((per, LANES), jnp.float32),
        ],
        compiler_params=params(32),
        cost_estimate=pl.CostEstimate(
            flops=0, bytes_accessed=60 * MIB, transcendentals=0
        ),
        name="send_rows",
    )(index, displacement)


def unpack_rows(per, packed_ref, rows_ref):
    slots = rows_ref.shape[0]
    quarter = per // 4
    lane = lax.broadcasted_iota(jnp.int32, (quarter, LANES), 1)

    def peer(d, carry):
        parts = []
        for i in range(3):
            at = pl.multiple_of(d * 3 * quarter + i * quarter, quarter)
            piece = packed_ref[pl.ds(at, quarter), :].astype(jnp.float32)
            parts.append(pltpu.roll(piece, 32 * (i + 1), 1))
            to = pl.multiple_of(d * per + i * quarter, quarter)
            rows_ref[pl.ds(to, quarter), :] = piece
        last = jnp.where(lane < 32, parts[0], jnp.where(lane < 64, parts[1], parts[2]))
        to = pl.multiple_of(d * per + 3 * quarter, quarter)
        rows_ref[pl.ds(to, quarter), :] = last
        return carry

    lax.fori_loop(0, slots // per, peer, 0)


def splits(x):
    high = x.astype(jnp.bfloat16).astype(jnp.float32)
    rest = x - high
    middle = rest.astype(jnp.bfloat16).astype(jnp.float32)
    return high, middle, rest - middle


def distance_rows(xyz, entry_side):
    rows = []
    square = None
    for c in range(3):
        x = xyz[c : c + 1, :] * (1.0 / KERNEL_RADIUS)
        square = x * x if square is None else square + x * x
        if entry_side:
            s1, s2, s3 = splits(-2.0 * x)
            rows += [s1, s1, s2, s2, s1, s3]
        else:
            p1, p2, p3 = splits(x)
            rows += [p1, p2, p1, p2, p3, p1]
    one = jnp.ones_like(square)
    own = list(splits(square))
    rows += own + [one] * 3 if entry_side else [one] * 3 + own
    rows += [jnp.zeros_like(square)] * 8
    return jnp.concatenate(rows, axis=0)


def falloff_terms(scaled_sq):
    safe = jnp.maximum(scaled_sq, 1e-12)
    return jnp.maximum(1.0 - safe * lax.rsqrt(safe), 0.0)


PANEL_CHUNK = 2048


def blend_kernel(
    support_count,
    points_ref,
    member_ref,
    centers_ref,
    support_ref,
    out_ref,
    panel_rows,
    five_ref,
    four_ref,
):
    panels = points_ref.shape[1]
    patches = centers_ref.shape[0]
    entries = support_ref.shape[1]
    block_patches = entries // support_count
    step = pl.program_id(0)

    @pl.when(step == 0)
    def _():
        panel_rows[...] = distance_rows(points_ref[...], False).astype(jnp.bfloat16)
        patch = lax.broadcasted_iota(jnp.int32, (patches, LANES), 0)

        def weigh(b, carry):
            at = pl.multiple_of(b * LANES, LANES)
            square = None
            for c in range(3):
                gap = centers_ref[:, c : c + 1] - points_ref[c : c + 1, pl.ds(at, LANES)]
                square = gap * gap if square is None else square + gap * gap
            u = falloff_terms(square * (1.0 / ATTRACTION_REACH**2))
            u2 = u * u
            owner = jnp.where(member_ref[:, pl.ds(at, LANES)] == patch, OWNER_PREMIUM, 0.0)
            attraction = u2 * u2 * (5.0 - 4.0 * u) + owner
            weight = attraction / jnp.sum(attraction, axis=0, keepdims=True)
            five_ref[:, pl.ds(at, LANES)] = 5.0 * weight
            four_ref[:, pl.ds(at, LANES)] = 4.0 * weight
            return carry

        lax.fori_loop(0, panels // LANES, weigh, 0)

    entry_rows = distance_rows(support_ref[...], True).T.astype(jnp.bfloat16)

    def chunk(b, carry):
        at = pl.multiple_of(b * PANEL_CHUNK, PANEL_CHUNK)
        first = pl.multiple_of(step * block_patches, block_patches)
        five = five_ref[pl.ds(first, block_patches), pl.ds(at, PANEL_CHUNK)]
        four = four_ref[pl.ds(first, block_patches), pl.ds(at, PANEL_CHUNK)]
        columns = panel_rows[:, pl.ds(at, PANEL_CHUNK)]
        whole = jnp.dot(entry_rows, columns, preferred_element_type=jnp.float32)
        for p in range(block_patches):
            rows = slice(p * support_count, (p + 1) * support_count)
            square = whole[rows]
            u = falloff_terms(square)
            u2 = u * u
            value = u2 * u2 * (five[p : p + 1] - four[p : p + 1] * u)
            out_ref[rows, pl.ds(at, PANEL_CHUNK)] = value.astype(jnp.bfloat16)
        return carry

    lax.fori_loop(0, panels // PANEL_CHUNK, chunk, 0)


def blend_entry_major(points, member, support_xyz, centers, support_count):
    panels = points.shape[1]
    patches = centers.shape[1]
    slots = support_xyz.shape[1]
    block = 8 * support_count
    return pl.pallas_call(
        functools.partial(blend_kernel, support_count),
        grid=(slots // block,),
        in_specs=[
            pl.BlockSpec((3, panels), lambda i: (0, 0)),
            pl.BlockSpec((1, panels), lambda i: (0, 0)),
            pl.BlockSpec((patches, 3), lambda i: (0, 0)),
            pl.BlockSpec((3, block), lambda i: (0, i)),
        ],
        out_specs=pl.BlockSpec((block, panels), lambda i: (i, 0)),
        out_shape=jax.ShapeDtypeStruct((slots, panels), jnp.bfloat16),
        scratch_shapes=[
            pltpu.VMEM((32, panels), jnp.bfloat16),
            pltpu.VMEM((patches, panels), jnp.float32),
            pltpu.VMEM((patches, panels), jnp.float32),
        ],
        compiler_params=params(40),
        cost_estimate=pl.CostEstimate(
            flops=64 * slots * panels,
            bytes_accessed=4 * slots * panels,
            transcendentals=slots * panels,
        ),
        name="blend",
    )(points, member.reshape(1, panels), centers.T, support_xyz)


BLOCK_PATCHES = 16


def moved_kernel(modes, per, support_count, groups, group_ref, index_ref, *refs):
    packed_ref, blend_ref, normals_ref = refs[:3]
    inverse_refs = refs[3 : 3 + groups]
    out_ref, rows_ref, picked_ref, values_ref, turned_ref, coef_ref, total_ref = refs[3 + groups :]
    step = pl.program_id(0)
    steps = pl.num_programs(0) - 1
    block = picked_ref.shape[0]

    @pl.when(step == 0)
    def _():
        total_ref[...] = jnp.zeros_like(total_ref)
        values_ref[...] = jnp.zeros_like(values_ref)
        unpack_rows(per, packed_ref, rows_ref)

    block_patches, width = inverse_refs[0].shape
    halves = width // LANES
    per_patch = groups * halves
    for k in range(groups):
        owner = lax.rem(group_ref[0] + groups - k, groups)
        for a in range(halves):
            piece = inverse_refs[k][:, a * LANES : (a + 1) * LANES].astype(jnp.float32)
            turned_ref[pl.ds(owner * halves + a, block_patches, stride=per_patch), :] = piece
    lane = lax.broadcasted_iota(jnp.int32, (8, LANES), 1)
    low = lane < support_count
    for pair in range(block_patches // 2):
        rows = []
        for side in range(2):
            for v in range(per_patch // 8):
                at = (2 * pair + side) * per_patch + 8 * v
                own = turned_ref[at : at + 8, :]
                other = pltpu.roll(own, support_count, 1)
                both = (own, other) if side == 0 else (other, own)
                keep = low if side == 0 else jnp.logical_not(low)
                rows += [jnp.where(keep, x, 0.0) for x in both]
        product = jnp.concatenate(rows, axis=0).astype(jnp.bfloat16)
        at = pair * LANES
        coef = jnp.dot(
            product, values_ref[at : at + LANES, :], preferred_element_type=jnp.float32
        )
        coef_ref[:, at : at + LANES] = coef.T[: 3 * modes].astype(jnp.bfloat16)
    total_ref[...] += jnp.dot(
        coef_ref[...], blend_ref[...], preferred_element_type=jnp.float32
    )

    base = jnp.minimum(step, steps - 1) * block
    for r in range(block):
        picked_ref[r : r + 1, :] = rows_ref[pl.ds(index_ref[base + r], 1), :]
    values_ref[...] = picked_ref[...].astype(jnp.bfloat16)

    @pl.when(step == steps)
    def _():
        result = None
        for c in range(3):
            term = normals_ref[c : c + 1, :] * total_ref[c * modes : (c + 1) * modes, :]
            result = term if result is None else result + term
        out_ref[...] = result


def moved_normals(group, index, packed, per, inverses, blend, normals, modes, support_count):
    groups = len(inverses)
    patches, width = inverses[0].shape
    slots, panels = blend.shape
    steps = patches // BLOCK_PATCHES
    block = BLOCK_PATCHES * support_count

    def before(i):
        return jnp.maximum(i - 1, 0)

    return pl.pallas_call(
        functools.partial(moved_kernel, modes, per, support_count, groups),
        grid=(steps + 1,),
        in_specs=[
            pl.BlockSpec(memory_space=pltpu.SMEM),
            pl.BlockSpec(memory_space=pltpu.SMEM),
            pl.BlockSpec(memory_space=pltpu.VMEM),
            pl.BlockSpec((block, panels), lambda i: (before(i), 0)),
            pl.BlockSpec((3, panels), lambda i: (0, 0)),
        ]
        + [pl.BlockSpec((BLOCK_PATCHES, width), lambda i: (before(i), 0))] * groups,
        out_specs=pl.BlockSpec((modes, panels), lambda i: (0, 0)),
        out_shape=jax.ShapeDtypeStruct((modes, panels), jnp.float32),
        scratch_shapes=[
            pltpu.VMEM((slots, LANES), jnp.float32),
            pltpu.VMEM((block, LANES), jnp.float32),
            pltpu.VMEM((block, LANES), jnp.bfloat16),
            pltpu.VMEM((block // 2, LANES), jnp.float32),
            pltpu.VMEM((3 * modes, block), jnp.bfloat16),
            pltpu.VMEM((3 * modes, panels), jnp.float32),
        ],
        compiler_params=params(48),
        cost_estimate=pl.CostEstimate(
            flops=2 * 3 * modes * panels * slots,
            bytes_accessed=2 * panels * slots,
            transcendentals=0,
        ),
        name="moved_normals",
    )(group.reshape(1), index, packed, blend, normals, *inverses)


def shards(

    displacement,
    send_index,
    support,
    support_xyz,
    patch_kernel_inverse,
    panel_xyz,
    normals,
    centers,
    member,
):
    axes = ("panel", "group")
    columns = displacement.shape[0]
    modes = columns // 3
    slots = send_index.shape[1]
    patches = centers.shape[1]
    support_count = slots // patches
    devices = lax.axis_size(axes)
    per = slots // devices
    own_rows = patch_kernel_inverse.shape[0]
    order = inverse_order(own_rows, support_count)
    if not np.array_equal(order, np.arange(support_count)):
        xyz = support_xyz.reshape(3, patches, support_count)
        support_xyz = jnp.take(xyz, order, axis=2).reshape(3, slots)

    groups = lax.axis_size("group")
    group = lax.axis_index("group")
    packs = [
        inverse_pack(patch_kernel_inverse, lax.rem(group + k, groups), patches)
        for k in range(groups)
    ]
    *packs, displacement = lax.optimization_barrier((*packs, displacement))
    inverses = [packs[0]]
    for k in range(1, groups):
        ring = [(i, (i + k) % groups) for i in range(groups)]
        inverses.append(lax.ppermute(packs[k], "group", ring))
    outgoing = send_rows(displacement, send_index.reshape(slots), per)
    outgoing, panel_xyz, inverses[1], inverses[-1] = lax.optimization_barrier(
        (outgoing, panel_xyz, inverses[1], inverses[-1])
    )
    arriving = lax.all_to_all(
        outgoing.reshape(devices, per * 3 // 4, LANES), axes, 0, 0, tiled=True
    ).reshape(slots * 3 // 4, LANES)
    blend = blend_entry_major(panel_xyz, member, support_xyz, centers, support_count)
    return moved_normals(
        group, support.reshape(slots), arriving, per, inverses, blend, normals, modes, support_count
    )


def solution(mesh):
    return jax.shard_map(
        shards,
        mesh=mesh,
        in_specs=(
            P(None, ("panel", "group")),
            P(("panel", "group"), None),
            P(("panel", "group"), None),
            P(None, ("panel", "group")),
            P("group", None, "panel"),
            P(None, ("panel", "group")),
            P(None, ("panel", "group")),
            P(None, ("panel", "group")),
            P(("panel", "group")),
        ),
        out_specs=P(None, ("panel", "group")),
        check_vma=False,
    )
```

```python
import functools

import jax
import jax.numpy as jnp
import numpy as np
from jax import lax
from jax.experimental import pallas as pl
from jax.experimental.pallas import tpu as pltpu
from jax.sharding import PartitionSpec as P

KERNEL_RADIUS = 0.45
ATTRACTION_REACH = 0.3
OWNER_PREMIUM = 8.0
LANES = 128
MIB = 1024 * 1024


def params(mib):
    return pltpu.CompilerParams(vmem_limit_bytes=mib * MIB)


def inverse_pack_kernel(window_ref, inverse_ref, out_ref):
    half = inverse_ref.shape[0] // 2
    for a in range(half):
        pair = jnp.concatenate([inverse_ref[a], inverse_ref[a + half]], axis=0)
        turned = pair.astype(jnp.float32).T
        out_ref[:, a * LANES : (a + 1) * LANES] = turned.astype(jnp.bfloat16)


def inverse_pack(inverse, window, patches):
    rows, support_count, _ = inverse.shape
    parts = patches // LANES
    width = rows * support_count
    return pl.pallas_call(
        inverse_pack_kernel,
        grid_spec=pltpu.PrefetchScalarGridSpec(
            num_scalar_prefetch=1,
            grid=(parts,),
            in_specs=[
                pl.BlockSpec(
                    (rows, support_count, LANES), lambda i, w: (0, 0, parts * w[0] + i)
                )
            ],
            out_specs=pl.BlockSpec((LANES, width), lambda i, w: (i, 0)),
        ),
        out_shape=jax.ShapeDtypeStruct((patches, width), jnp.bfloat16),
        compiler_params=params(24),
        cost_estimate=pl.CostEstimate(
            flops=0, bytes_accessed=4 * patches * width, transcendentals=0
        ),
        name="inverse_pack",
    )(window.reshape(1), inverse)


def inverse_order(rows, support_count):
    half = rows // 2
    order = []
    for v in range(support_count // 16):
        for side in range(2):
            for i in range(8):
                r = 8 * v + i
                order.append((r // half) * rows + side * half + r % half)
    return np.array(order)


UNROLL = 128


def gather_rows(index_ref, source, target, base, count):
    def body(step, carry):
        for r in range(UNROLL):
            at = step * UNROLL + r
            target[pl.ds(at, 1), :] = source[pl.ds(index_ref[base + at], 1), :]
        return carry

    lax.fori_loop(0, count // UNROLL, body, 0)


def send_kernel(per, index_ref, displacement_ref, out_ref, rows_ref, block_ref):
    columns, nodes = displacement_ref.shape

    def turn(block, carry):
        at = pl.multiple_of(block * LANES, LANES)
        piece = displacement_ref[:, pl.ds(at, LANES)].astype(jnp.float32)
        piece = jnp.concatenate([piece, piece[: LANES - columns]], axis=0)
        rows_ref[pl.ds(at, LANES), :] = piece.T
        return carry

    lax.fori_loop(0, nodes // LANES, turn, 0, unroll=4)
    quarter = per // 4
    lane = lax.broadcasted_iota(jnp.int32, (quarter, LANES), 1)

    def peer(d, carry):
        gather_rows(index_ref, rows_ref, block_ref, d * per, per)
        last = block_ref[3 * quarter : 4 * quarter, :]
        for i in range(3):
            own = block_ref[i * quarter : (i + 1) * quarter, :]
            full = jnp.where(lane < 96, own, pltpu.roll(last, 96 - 32 * i, 1))
            at = pl.multiple_of(d * 3 * quarter + i * quarter, quarter)
            out_ref[pl.ds(at, quarter), :] = full.astype(jnp.bfloat16)
        return carry

    lax.fori_loop(0, nodes // per, peer, 0)


def send_rows(displacement, index, per):
    columns, nodes = displacement.shape
    return pl.pallas_call(
        functools.partial(send_kernel, per),
        in_specs=[
            pl.BlockSpec(memory_space=pltpu.SMEM),
            pl.BlockSpec(memory_space=pltpu.VMEM),
        ],
        out_specs=pl.BlockSpec(memory_space=pltpu.VMEM),
        out_shape=jax.ShapeDtypeStruct((nodes * 3 // 4, LANES), jnp.bfloat16),
        scratch_shapes=[
            pltpu.VMEM((nodes, LANES), jnp.float32),
            pltpu.VMEM((per, LANES), jnp.float32),
        ],
        compiler_params=params(32),
        cost_estimate=pl.CostEstimate(
            flops=0, bytes_accessed=60 * MIB, transcendentals=0
        ),
        name="send_rows",
    )(index, displacement)


def unpack_rows(per, packed_ref, rows_ref):
    slots = rows_ref.shape[0]
    quarter = per // 4
    lane = lax.broadcasted_iota(jnp.int32, (quarter, LANES), 1)

    def peer(d, carry):
        parts = []
        for i in range(3):
            at = pl.multiple_of(d * 3 * quarter + i * quarter, quarter)
            piece = packed_ref[pl.ds(at, quarter), :].astype(jnp.float32)
            parts.append(pltpu.roll(piece, 32 * (i + 1), 1))
            to = pl.multiple_of(d * per + i * quarter, quarter)
            rows_ref[pl.ds(to, quarter), :] = piece
        last = jnp.where(lane < 32, parts[0], jnp.where(lane < 64, parts[1], parts[2]))
        to = pl.multiple_of(d * per + 3 * quarter, quarter)
        rows_ref[pl.ds(to, quarter), :] = last
        return carry

    lax.fori_loop(0, slots // per, peer, 0)


def splits(x):
    high = x.astype(jnp.bfloat16).astype(jnp.float32)
    rest = x - high
    middle = rest.astype(jnp.bfloat16).astype(jnp.float32)
    return high, middle, rest - middle


def distance_rows(xyz, entry_side):
    rows = []
    square = None
    for c in range(3):
        x = xyz[c : c + 1, :] * (1.0 / KERNEL_RADIUS)
        square = x * x if square is None else square + x * x
        if entry_side:
            s1, s2, s3 = splits(-2.0 * x)
            rows += [s1, s1, s2, s2, s1, s3]
        else:
            p1, p2, p3 = splits(x)
            rows += [p1, p2, p1, p2, p3, p1]
    one = jnp.ones_like(square)
    own = list(splits(square))
    rows += own + [one] * 3 if entry_side else [one] * 3 + own
    rows += [jnp.zeros_like(square)] * 8
    return jnp.concatenate(rows, axis=0)


def falloff_terms(scaled_sq):
    safe = jnp.maximum(scaled_sq, 1e-12)
    return jnp.maximum(1.0 - safe * lax.rsqrt(safe), 0.0)


PANEL_CHUNK = 2048
SPAN = 16
EARLY = 1


def blend_kernel(
    support_count, first_step, points_ref, member_ref, centers_ref, support_ref, *refs
):
    out_ref, panel_rows, five_ref, four_ref = refs[-4:]
    panels = points_ref.shape[1]
    patches = centers_ref.shape[0]
    entries = support_ref.shape[1]
    block_patches = entries // support_count
    step = pl.program_id(0)

    @pl.when(step == 0)
    def _():
        panel_rows[...] = distance_rows(points_ref[...], False).astype(jnp.bfloat16)
        patch = lax.broadcasted_iota(jnp.int32, (patches, LANES), 0)

        def weigh(b, carry):
            at = pl.multiple_of(b * LANES, LANES)
            square = None
            for c in range(3):
                gap = centers_ref[:, c : c + 1] - points_ref[c : c + 1, pl.ds(at, LANES)]
                square = gap * gap if square is None else square + gap * gap
            u = falloff_terms(square * (1.0 / ATTRACTION_REACH**2))
            u2 = u * u
            owner = jnp.where(member_ref[:, pl.ds(at, LANES)] == patch, OWNER_PREMIUM, 0.0)
            attraction = u2 * u2 * (5.0 - 4.0 * u) + owner
            weight = attraction / jnp.sum(attraction, axis=0, keepdims=True)
            five_ref[:, pl.ds(at, LANES)] = 5.0 * weight
            four_ref[:, pl.ds(at, LANES)] = 4.0 * weight
            return carry

        lax.fori_loop(0, panels // LANES, weigh, 0)

    entry_rows = distance_rows(support_ref[...], True).T.astype(jnp.bfloat16)

    def chunk(b, carry):
        at = pl.multiple_of(b * PANEL_CHUNK, PANEL_CHUNK)
        first = pl.multiple_of((first_step + step) * block_patches, block_patches)
        five = five_ref[pl.ds(first, block_patches), pl.ds(at, PANEL_CHUNK)]
        four = four_ref[pl.ds(first, block_patches), pl.ds(at, PANEL_CHUNK)]
        columns = panel_rows[:, pl.ds(at, PANEL_CHUNK)]
        whole = jnp.dot(entry_rows, columns, preferred_element_type=jnp.float32)
        for p in range(block_patches):
            rows = slice(p * support_count, (p + 1) * support_count)
            square = whole[rows]
            u = falloff_terms(square)
            u2 = u * u
            value = u2 * u2 * (five[p : p + 1] - four[p : p + 1] * u)
            out_ref[rows, pl.ds(at, PANEL_CHUNK)] = value.astype(jnp.bfloat16)
        return carry

    lax.fori_loop(0, panels // PANEL_CHUNK, chunk, 0)


def blend_entry_major(points, member, support_xyz, centers, support_count, span, begun=None):
    panels = points.shape[1]
    patches = centers.shape[1]
    slots = support_xyz.shape[1]
    block = 8 * support_count
    low, high = (slots * x // (block * SPAN) for x in span)
    more = [] if begun is None else [begun]
    return pl.pallas_call(
        functools.partial(blend_kernel, support_count, low),
        grid=(high - low,),
        in_specs=[
            pl.BlockSpec((3, panels), lambda i: (0, 0)),
            pl.BlockSpec((1, panels), lambda i: (0, 0)),
            pl.BlockSpec((patches, 3), lambda i: (0, 0)),
            pl.BlockSpec((3, block), lambda i: (0, low + i)),
        ]
        + [pl.BlockSpec(memory_space=pl.ANY)] * len(more),
        out_specs=pl.BlockSpec((block, panels), lambda i: (low + i, 0)),
        out_shape=jax.ShapeDtypeStruct((slots, panels), jnp.bfloat16),
        scratch_shapes=[
            pltpu.VMEM((32, panels), jnp.bfloat16),
            pltpu.VMEM((patches, panels), jnp.float32),
            pltpu.VMEM((patches, panels), jnp.float32),
        ],
        compiler_params=params(60),
        cost_estimate=pl.CostEstimate(
            flops=64 * (high - low) * block * panels,
            bytes_accessed=4 * (high - low) * block * panels,
            transcendentals=(high - low) * block * panels,
        ),
        input_output_aliases={4: 0} if more else {},
        name="blend",
    )(points, member.reshape(1, panels), centers.T, support_xyz, *more)


BLOCK_PATCHES = 16
BLEND_DEPTH = 6


def products_kernel(support_count, groups, group_ref, *refs):
    inverse_refs = refs[:groups]
    out_ref, turned_ref = refs[groups:]
    block_patches, width = inverse_refs[0].shape
    halves = width // LANES
    per_patch = groups * halves
    for k in range(groups):
        owner = lax.rem(group_ref[0] + groups - k, groups)
        for a in range(halves):
            piece = inverse_refs[k][:, a * LANES : (a + 1) * LANES].astype(jnp.float32)
            turned_ref[pl.ds(owner * halves + a, block_patches, stride=per_patch), :] = piece
    lane = lax.broadcasted_iota(jnp.int32, (8, LANES), 1)
    low = lane < support_count
    for pair in range(block_patches // 2):
        rows = []
        for side in range(2):
            for v in range(per_patch // 8):
                at = (2 * pair + side) * per_patch + 8 * v
                own = turned_ref[at : at + 8, :]
                other = pltpu.roll(own, support_count, 1)
                both = (own, other) if side == 0 else (other, own)
                keep = low if side == 0 else jnp.logical_not(low)
                rows += [jnp.where(keep, x, 0.0) for x in both]
        product = jnp.concatenate(rows, axis=0).astype(jnp.bfloat16)
        out_ref[pair * LANES : (pair + 1) * LANES, :] = product


def pair_products(group, inverses, support_count):
    groups = len(inverses)
    patches, width = inverses[0].shape
    block = BLOCK_PATCHES * support_count
    return pl.pallas_call(
        functools.partial(products_kernel, support_count, groups),
        grid=(patches // BLOCK_PATCHES,),
        in_specs=[pl.BlockSpec(memory_space=pltpu.SMEM)]
        + [pl.BlockSpec((BLOCK_PATCHES, width), lambda i: (i, 0))] * groups,
        out_specs=pl.BlockSpec((block, LANES), lambda i: (i, 0)),
        out_shape=jax.ShapeDtypeStruct((patches * support_count, LANES), jnp.bfloat16),
        scratch_shapes=[pltpu.VMEM((block // 2, LANES), jnp.float32)],
        compiler_params=params(60),
        cost_estimate=pl.CostEstimate(
            flops=0, bytes_accessed=20 * MIB, transcendentals=0
        ),
        name="pair_products",
    )(group.reshape(1), *inverses)


def moved_kernel(modes, per, index_ref, packed_ref, products_ref, blend_ref, normals_ref, *refs):
    out_ref, rows_ref, picked_ref, values_ref, coef_ref, summed_ref = refs[:6]
    total_ref, blend_slots, arrived = refs[6:]
    step = pl.program_id(0)
    steps = pl.num_programs(0) - 2
    block = picked_ref.shape[0]
    depth = blend_slots.shape[0]

    def fetch(b):
        return pltpu.make_async_copy(
            blend_ref.at[pl.ds(pl.multiple_of(b * block, block), block), :],
            blend_slots.at[lax.rem(b, depth)],
            arrived.at[lax.rem(b, depth)],
        )

    @pl.when(step == 0)
    def _():
        for b in range(depth):
            fetch(b).start()
        total_ref[...] = jnp.zeros_like(total_ref)
        values_ref[...] = jnp.zeros_like(values_ref)
        coef_ref[...] = jnp.zeros_like(coef_ref)
        unpack_rows(per, packed_ref, rows_ref)
        fetch(0).wait()

    @pl.when(step >= 3)
    def _():
        fetch(step - 2).wait()

        @pl.when(step - 3 + depth < steps)
        def _():
            fetch(step - 3 + depth).start()

    summed_ref[...] = coef_ref[...]
    slot = lax.rem(jnp.maximum(step - 2, 0), depth)
    base = jnp.minimum(step, steps - 1) * block
    pairs = block // LANES
    tile = total_ref.shape[1] // pairs
    for pair in range(pairs):
        columns = slice(pair * tile, (pair + 1) * tile)
        total_ref[:, columns] += jnp.dot(
            summed_ref[...], blend_slots[slot, :, columns], preferred_element_type=jnp.float32
        )
        for r in range(pair * LANES, (pair + 1) * LANES):
            picked_ref[r : r + 1, :] = rows_ref[pl.ds(index_ref[base + r], 1), :]
        at = pair * LANES
        coef = jnp.dot(
            products_ref[at : at + LANES, :],
            values_ref[at : at + LANES, :],
            preferred_element_type=jnp.float32,
        )
        coef_ref[:, at : at + LANES] = coef.T[: 3 * modes].astype(jnp.bfloat16)
    values_ref[...] = picked_ref[...].astype(jnp.bfloat16)

    @pl.when(step == steps + 1)
    def _():
        result = None
        for c in range(3):
            term = normals_ref[c : c + 1, :] * total_ref[c * modes : (c + 1) * modes, :]
            result = term if result is None else result + term
        out_ref[...] = result


def moved_normals(index, packed, per, products, blend, normals, modes):
    slots, panels = blend.shape
    block = BLOCK_PATCHES * (LANES // 2)
    steps = slots // block

    def before(i):
        return jnp.clip(i - 1, 0, steps - 1)

    return pl.pallas_call(
        functools.partial(moved_kernel, modes, per),
        grid=(steps + 2,),
        in_specs=[
            pl.BlockSpec(memory_space=pltpu.SMEM),
            pl.BlockSpec(memory_space=pltpu.VMEM),
            pl.BlockSpec((block, LANES), lambda i: (before(i), 0)),
            pl.BlockSpec(memory_space=pl.ANY),
            pl.BlockSpec((3, panels), lambda i: (0, 0)),
        ],
        out_specs=pl.BlockSpec((modes, panels), lambda i: (0, 0)),
        out_shape=jax.ShapeDtypeStruct((modes, panels), jnp.float32),
        scratch_shapes=[
            pltpu.VMEM((slots, LANES), jnp.float32),
            pltpu.VMEM((block, LANES), jnp.float32),
            pltpu.VMEM((block, LANES), jnp.bfloat16),
            pltpu.VMEM((3 * modes, block), jnp.bfloat16),
            pltpu.VMEM((3 * modes, block), jnp.bfloat16),
            pltpu.VMEM((3 * modes, panels), jnp.float32),
            pltpu.VMEM((BLEND_DEPTH, block, panels), jnp.bfloat16),
            pltpu.SemaphoreType.DMA((BLEND_DEPTH,)),
        ],
        compiler_params=params(60),
        cost_estimate=pl.CostEstimate(
            flops=2 * 3 * modes * panels * slots,
            bytes_accessed=2 * panels * slots,
            transcendentals=0,
        ),
        name="moved_normals",
    )(index, packed, products, blend, normals)


def shards(

    displacement,
    send_index,
    support,
    support_xyz,
    patch_kernel_inverse,
    panel_xyz,
    normals,
    centers,
    member,
):
    axes = ("panel", "group")
    columns = displacement.shape[0]
    modes = columns // 3
    slots = send_index.shape[1]
    patches = centers.shape[1]
    support_count = slots // patches
    devices = lax.axis_size(axes)
    per = slots // devices
    own_rows = patch_kernel_inverse.shape[0]
    order = inverse_order(own_rows, support_count)
    if not np.array_equal(order, np.arange(support_count)):
        xyz = support_xyz.reshape(3, patches, support_count)
        support_xyz = jnp.take(xyz, order, axis=2).reshape(3, slots)

    groups = lax.axis_size("group")
    group = lax.axis_index("group")
    packs = [
        inverse_pack(patch_kernel_inverse, lax.rem(group + k, groups), patches)
        for k in range(groups)
    ]
    inverses = [packs[0]]
    for k in range(1, groups):
        ring = [(i, (i + k) % groups) for i in range(groups)]
        inverses.append(lax.ppermute(packs[k], "group", ring))
    outgoing = send_rows(displacement, send_index.reshape(slots), per)
    shape = (panel_xyz, member, support_xyz, centers)
    blend = blend_entry_major(*shape, support_count, (0, EARLY))
    outgoing, blend, inverses = lax.optimization_barrier((outgoing, blend, inverses))
    arriving = lax.all_to_all(
        outgoing.reshape(devices, per * 3 // 4, LANES), axes, 0, 0, tiled=True
    ).reshape(slots * 3 // 4, LANES)
    products = pair_products(group, inverses, support_count)
    blend = blend_entry_major(*shape, support_count, (EARLY, SPAN), blend)
    return moved_normals(
        support.reshape(slots), arriving, per, products, blend, normals, modes
    )


def solution(mesh):
    return jax.shard_map(
        shards,
        mesh=mesh,
        in_specs=(
            P(None, ("panel", "group")),
            P(("panel", "group"), None),
            P(("panel", "group"), None),
            P(None, ("panel", "group")),
            P("group", None, "panel"),
            P(None, ("panel", "group")),
            P(None, ("panel", "group")),
            P(None, ("panel", "group")),
            P(("panel", "group")),
        ),
        out_specs=P(None, ("panel", "group")),
        check_vma=False,
    )
```

```python
import functools

import jax
import jax.numpy as jnp
import numpy as np
from jax import lax
from jax.experimental import pallas as pl
from jax.experimental.pallas import tpu as pltpu
from jax.sharding import PartitionSpec as P

KERNEL_RADIUS = 0.45
ATTRACTION_REACH = 0.3
OWNER_PREMIUM = 8.0
LANES = 128
MIB = 1024 * 1024


def params(mib):
    return pltpu.CompilerParams(vmem_limit_bytes=mib * MIB)


def inverse_pack_kernel(window_ref, inverse_ref, out_ref):
    half = inverse_ref.shape[0] // 2
    for a in range(half):
        pair = jnp.concatenate([inverse_ref[a], inverse_ref[a + half]], axis=0)
        turned = pair.astype(jnp.float32).T
        out_ref[:, a * LANES : (a + 1) * LANES] = turned.astype(jnp.bfloat16)


def inverse_pack(inverse, window, patches):
    rows, support_count, _ = inverse.shape
    parts = patches // LANES
    width = rows * support_count
    return pl.pallas_call(
        inverse_pack_kernel,
        grid_spec=pltpu.PrefetchScalarGridSpec(
            num_scalar_prefetch=1,
            grid=(parts,),
            in_specs=[
                pl.BlockSpec(
                    (rows, support_count, LANES), lambda i, w: (0, 0, parts * w[0] + i)
                )
            ],
            out_specs=pl.BlockSpec((LANES, width), lambda i, w: (i, 0)),
        ),
        out_shape=jax.ShapeDtypeStruct((patches, width), jnp.bfloat16),
        compiler_params=params(24),
        cost_estimate=pl.CostEstimate(
            flops=0, bytes_accessed=4 * patches * width, transcendentals=0
        ),
        name="inverse_pack",
    )(window.reshape(1), inverse)


def inverse_order(rows, support_count):
    half = rows // 2
    order = []
    for v in range(support_count // 16):
        for side in range(2):
            for i in range(8):
                r = 8 * v + i
                order.append((r // half) * rows + side * half + r % half)
    return np.array(order)


UNROLL = 128
PIECES = 4


def gather_rows(index_ref, source, target, base, count):
    def body(step, carry):
        for r in range(UNROLL):
            at = step * UNROLL + r
            target[pl.ds(at, 1), :] = source[pl.ds(index_ref[base + at], 1), :]
        return carry

    lax.fori_loop(0, count // UNROLL, body, 0)


def send_kernel(
    per, index_ref, source_ref, out_ref, rows_ref, block_ref, displacement_ref, arrived
):
    columns, nodes = displacement_ref.shape
    piece_nodes = nodes // PIECES

    def fetch(i):
        span = pl.ds(i * piece_nodes, piece_nodes)
        return pltpu.make_async_copy(
            source_ref.at[:, span], displacement_ref.at[:, span], arrived.at[i]
        )

    for i in range(PIECES):
        fetch(i).start()

    def turn(block, carry):
        at = pl.multiple_of(block * LANES, LANES)
        piece = displacement_ref[:, pl.ds(at, LANES)].astype(jnp.float32)
        piece = jnp.concatenate([piece, piece[: LANES - columns]], axis=0)
        rows_ref[pl.ds(at, LANES), :] = piece.T
        return carry

    blocks = piece_nodes // LANES
    for i in range(PIECES):
        fetch(i).wait()
        lax.fori_loop(i * blocks, (i + 1) * blocks, turn, 0, unroll=4)
    quarter = per // 4
    lane = lax.broadcasted_iota(jnp.int32, (quarter, LANES), 1)

    def peer(d, carry):
        gather_rows(index_ref, rows_ref, block_ref, d * per, per)
        last = block_ref[3 * quarter : 4 * quarter, :]
        for i in range(3):
            own = block_ref[i * quarter : (i + 1) * quarter, :]
            full = jnp.where(lane < 96, own, pltpu.roll(last, 96 - 32 * i, 1))
            at = pl.multiple_of(d * 3 * quarter + i * quarter, quarter)
            out_ref[pl.ds(at, quarter), :] = full.astype(jnp.bfloat16)
        return carry

    lax.fori_loop(0, nodes // per, peer, 0)


def send_rows(displacement, index, per):
    columns, nodes = displacement.shape
    return pl.pallas_call(
        functools.partial(send_kernel, per),
        in_specs=[
            pl.BlockSpec(memory_space=pltpu.SMEM),
            pl.BlockSpec(memory_space=pl.ANY),
        ],
        out_specs=pl.BlockSpec(memory_space=pltpu.VMEM),
        out_shape=jax.ShapeDtypeStruct((nodes * 3 // 4, LANES), jnp.bfloat16),
        scratch_shapes=[
            pltpu.VMEM((nodes, LANES), jnp.float32),
            pltpu.VMEM((per, LANES), jnp.float32),
            pltpu.VMEM((columns, nodes), jnp.bfloat16),
            pltpu.SemaphoreType.DMA((PIECES,)),
        ],
        compiler_params=params(56),
        cost_estimate=pl.CostEstimate(
            flops=0, bytes_accessed=60 * MIB, transcendentals=0
        ),
        name="send_rows",
    )(index, displacement)


def unpack_rows(per, packed_ref, rows_ref, first, end):
    quarter = per // 4
    lane = lax.broadcasted_iota(jnp.int32, (quarter, LANES), 1)

    def peer(d, carry):
        parts = []
        for i in range(3):
            at = pl.multiple_of(d * 3 * quarter + i * quarter, quarter)
            piece = packed_ref[pl.ds(at, quarter), :].astype(jnp.float32)
            parts.append(pltpu.roll(piece, 32 * (i + 1), 1))
            to = pl.multiple_of(d * per + i * quarter, quarter)
            rows_ref[pl.ds(to, quarter), :] = piece
        last = jnp.where(lane < 32, parts[0], jnp.where(lane < 64, parts[1], parts[2]))
        to = pl.multiple_of(d * per + 3 * quarter, quarter)
        rows_ref[pl.ds(to, quarter), :] = last
        return carry

    lax.fori_loop(first, end, peer, 0)


def splits(x):
    high = x.astype(jnp.bfloat16).astype(jnp.float32)
    rest = x - high
    middle = rest.astype(jnp.bfloat16).astype(jnp.float32)
    return high, middle, rest - middle


def distance_rows(xyz, entry_side):
    rows = []
    square = None
    for c in range(3):
        x = xyz[c : c + 1, :] * (1.0 / KERNEL_RADIUS)
        square = x * x if square is None else square + x * x
        if entry_side:
            s1, s2, s3 = splits(-2.0 * x)
            rows += [s1, s1, s2, s2, s1, s3]
        else:
            p1, p2, p3 = splits(x)
            rows += [p1, p2, p1, p2, p3, p1]
    one = jnp.ones_like(square)
    own = list(splits(square))
    rows += own + [one] * 3 if entry_side else [one] * 3 + own
    rows += [jnp.zeros_like(square)] * 8
    return jnp.concatenate(rows, axis=0)


def falloff_terms(scaled_sq):
    safe = jnp.maximum(scaled_sq, 1e-12)
    return jnp.maximum(1.0 - safe * lax.rsqrt(safe), 0.0)


PANEL_CHUNK = 2048


def weights_kernel(points_ref, member_ref, centers_ref, five_ref, four_ref):
    panels = points_ref.shape[1]
    patches = centers_ref.shape[0]
    patch = lax.broadcasted_iota(jnp.int32, (patches, LANES), 0)

    def weigh(b, carry):
        at = pl.multiple_of(b * LANES, LANES)
        square = None
        for c in range(3):
            gap = centers_ref[:, c : c + 1] - points_ref[c : c + 1, pl.ds(at, LANES)]
            square = gap * gap if square is None else square + gap * gap
        u = falloff_terms(square * (1.0 / ATTRACTION_REACH**2))
        u2 = u * u
        owner = jnp.where(member_ref[:, pl.ds(at, LANES)] == patch, OWNER_PREMIUM, 0.0)
        attraction = u2 * u2 * (5.0 - 4.0 * u) + owner
        weight = attraction / jnp.sum(attraction, axis=0, keepdims=True)
        five_ref[:, pl.ds(at, LANES)] = 5.0 * weight
        four_ref[:, pl.ds(at, LANES)] = 4.0 * weight
        return carry

    lax.fori_loop(0, panels // LANES, weigh, 0, unroll=2)


def panel_weights(points, member, centers):
    panels = points.shape[1]
    patches = centers.shape[1]
    tile = panels // 4
    shape = jax.ShapeDtypeStruct((patches, panels), jnp.float32)
    return pl.pallas_call(
        weights_kernel,
        grid=(panels // tile,),
        in_specs=[
            pl.BlockSpec((3, tile), lambda i: (0, i)),
            pl.BlockSpec((1, tile), lambda i: (0, i)),
            pl.BlockSpec((patches, 3), lambda i: (0, 0)),
        ],
        out_specs=[pl.BlockSpec((patches, tile), lambda i: (0, i))] * 2,
        out_shape=(shape, shape),
        compiler_params=params(60),
        cost_estimate=pl.CostEstimate(
            flops=20 * patches * panels,
            bytes_accessed=8 * patches * panels,
            transcendentals=patches * panels,
        ),
        name="panel_weights",
    )(points, member.reshape(1, panels), centers.T)


def blend_kernel(
    support_count, points_ref, five_ref, four_ref, support_ref, out_ref, panel_rows
):
    panels = points_ref.shape[1]
    block_patches = five_ref.shape[0]

    @pl.when(pl.program_id(0) == 0)
    def _():
        panel_rows[...] = distance_rows(points_ref[...], False).astype(jnp.bfloat16)

    entry_rows = distance_rows(support_ref[...], True).T.astype(jnp.bfloat16)

    def chunk(b, carry):
        at = pl.multiple_of(b * PANEL_CHUNK, PANEL_CHUNK)
        five = five_ref[:, pl.ds(at, PANEL_CHUNK)]
        four = four_ref[:, pl.ds(at, PANEL_CHUNK)]
        columns = panel_rows[:, pl.ds(at, PANEL_CHUNK)]
        whole = jnp.dot(entry_rows, columns, preferred_element_type=jnp.float32)
        for p in range(block_patches):
            rows = slice(p * support_count, (p + 1) * support_count)
            square = whole[rows]
            u = falloff_terms(square)
            u2 = u * u
            value = u2 * u2 * (five[p : p + 1] - four[p : p + 1] * u)
            out_ref[rows, pl.ds(at, PANEL_CHUNK)] = value.astype(jnp.bfloat16)
        return carry

    lax.fori_loop(0, panels // PANEL_CHUNK, chunk, 0)


def blend_entry_major(points, weights, support_xyz, support_count):
    panels = points.shape[1]
    slots = support_xyz.shape[1]
    block = 8 * support_count
    return pl.pallas_call(
        functools.partial(blend_kernel, support_count),
        grid=(slots // block,),
        in_specs=[
            pl.BlockSpec((3, panels), lambda i: (0, 0)),
            pl.BlockSpec((8, panels), lambda i: (i, 0)),
            pl.BlockSpec((8, panels), lambda i: (i, 0)),
            pl.BlockSpec((3, block), lambda i: (0, i)),
        ],
        out_specs=pl.BlockSpec((block, panels), lambda i: (i, 0)),
        out_shape=jax.ShapeDtypeStruct((slots, panels), jnp.bfloat16),
        scratch_shapes=[
            pltpu.VMEM((32, panels), jnp.bfloat16),
        ],
        compiler_params=params(60),
        cost_estimate=pl.CostEstimate(
            flops=64 * slots * panels,
            bytes_accessed=4 * slots * panels,
            transcendentals=slots * panels,
        ),
        name="blend",
    )(points, *weights, support_xyz)


BLOCK_PATCHES = 16
BLEND_DEPTH = 4
PRODUCT_PATCHES = 64


def products_kernel(support_count, groups, group_ref, *refs):
    inverse_refs = refs[:groups]
    out_ref, turned_ref = refs[groups:]
    block_patches, width = inverse_refs[0].shape
    halves = width // LANES
    per_patch = groups * halves
    for k in range(groups):
        owner = lax.rem(group_ref[0] + groups - k, groups)
        for a in range(halves):
            piece = inverse_refs[k][:, a * LANES : (a + 1) * LANES].astype(jnp.float32)
            turned_ref[pl.ds(owner * halves + a, block_patches, stride=per_patch), :] = piece
    lane = lax.broadcasted_iota(jnp.int32, (8, LANES), 1)
    low = lane < support_count
    for pair in range(block_patches // 2):
        rows = []
        for side in range(2):
            for v in range(per_patch // 8):
                at = (2 * pair + side) * per_patch + 8 * v
                own = turned_ref[at : at + 8, :]
                other = pltpu.roll(own, support_count, 1)
                both = (own, other) if side == 0 else (other, own)
                keep = low if side == 0 else jnp.logical_not(low)
                rows += [jnp.where(keep, x, 0.0) for x in both]
        product = jnp.concatenate(rows, axis=0).astype(jnp.bfloat16)
        out_ref[pair * LANES : (pair + 1) * LANES, :] = product


def pair_products(group, inverses, support_count):
    groups = len(inverses)
    patches, width = inverses[0].shape
    block = PRODUCT_PATCHES * support_count
    return pl.pallas_call(
        functools.partial(products_kernel, support_count, groups),
        grid=(patches // PRODUCT_PATCHES,),
        in_specs=[pl.BlockSpec(memory_space=pltpu.SMEM)]
        + [pl.BlockSpec((PRODUCT_PATCHES, width), lambda i: (i, 0))] * groups,
        out_specs=pl.BlockSpec((block, LANES), lambda i: (i, 0)),
        out_shape=jax.ShapeDtypeStruct((patches * support_count, LANES), jnp.bfloat16),
        scratch_shapes=[pltpu.VMEM((block // 2, LANES), jnp.float32)],
        compiler_params=params(60),
        cost_estimate=pl.CostEstimate(
            flops=0, bytes_accessed=20 * MIB, transcendentals=0
        ),
        name="pair_products",
    )(group.reshape(1), *inverses)


def moved_kernel(modes, per, index_ref, source_ref, products_ref, blend_ref, normals_ref, *refs):
    out_ref, rows_ref, picked_ref, values_ref, coef_ref, summed_ref = refs[:6]
    total_ref, blend_slots, arrived, packed_ref, landed = refs[6:]
    step = pl.program_id(0)
    steps = pl.num_programs(0) - 2
    block = picked_ref.shape[0]
    depth = blend_slots.shape[0]

    def fetch(b):
        return pltpu.make_async_copy(
            blend_ref.at[pl.ds(pl.multiple_of(b * block, block), block), :],
            blend_slots.at[lax.rem(b, depth)],
            arrived.at[lax.rem(b, depth)],
        )

    @pl.when(step == 0)
    def _():
        rows = packed_ref.shape[0] // PIECES
        pieces = []
        for i in range(PIECES):
            span = pl.ds(i * rows, rows)
            pieces.append(
                pltpu.make_async_copy(source_ref.at[span], packed_ref.at[span], landed.at[i])
            )
            pieces[i].start()
        for b in range(depth):
            fetch(b).start()
        total_ref[...] = jnp.zeros_like(total_ref)
        values_ref[...] = jnp.zeros_like(values_ref)
        coef_ref[...] = jnp.zeros_like(coef_ref)
        peers = rows_ref.shape[0] // (per * PIECES)
        for i in range(PIECES):
            pieces[i].wait()
            unpack_rows(per, packed_ref, rows_ref, i * peers, (i + 1) * peers)
        fetch(0).wait()

    @pl.when(step >= 3)
    def _():
        fetch(step - 2).wait()

        @pl.when(step - 3 + depth < steps)
        def _():
            fetch(step - 3 + depth).start()

    summed_ref[...] = coef_ref[...]
    slot = lax.rem(jnp.maximum(step - 2, 0), depth)
    base = jnp.minimum(step, steps - 1) * block
    pairs = block // LANES
    tile = total_ref.shape[1] // pairs
    for pair in range(pairs):
        columns = slice(pair * tile, (pair + 1) * tile)
        total_ref[:, columns] += jnp.dot(
            summed_ref[...], blend_slots[slot, :, columns], preferred_element_type=jnp.float32
        )
        for r in range(pair * LANES, (pair + 1) * LANES):
            picked_ref[r : r + 1, :] = rows_ref[pl.ds(index_ref[base + r], 1), :]
        at = pair * LANES
        coef = jnp.dot(
            products_ref[at : at + LANES, :],
            values_ref[at : at + LANES, :],
            preferred_element_type=jnp.float32,
        )
        coef_ref[:, at : at + LANES] = coef.T[: 3 * modes].astype(jnp.bfloat16)
    values_ref[...] = picked_ref[...].astype(jnp.bfloat16)

    @pl.when(step == steps + 1)
    def _():
        result = None
        for c in range(3):
            term = normals_ref[c : c + 1, :] * total_ref[c * modes : (c + 1) * modes, :]
            result = term if result is None else result + term
        out_ref[...] = result


def moved_normals(index, packed, per, products, blend, normals, modes):
    slots, panels = blend.shape
    block = BLOCK_PATCHES * (LANES // 2)
    steps = slots // block

    def before(i):
        return jnp.clip(i - 1, 0, steps - 1)

    return pl.pallas_call(
        functools.partial(moved_kernel, modes, per),
        grid=(steps + 2,),
        in_specs=[
            pl.BlockSpec(memory_space=pltpu.SMEM),
            pl.BlockSpec(memory_space=pl.ANY),
            pl.BlockSpec((block, LANES), lambda i: (before(i), 0)),
            pl.BlockSpec(memory_space=pl.ANY),
            pl.BlockSpec((3, panels), lambda i: (0, 0)),
        ],
        out_specs=pl.BlockSpec((modes, panels), lambda i: (0, 0)),
        out_shape=jax.ShapeDtypeStruct((modes, panels), jnp.float32),
        scratch_shapes=[
            pltpu.VMEM((slots, LANES), jnp.float32),
            pltpu.VMEM((block, LANES), jnp.float32),
            pltpu.VMEM((block, LANES), jnp.bfloat16),
            pltpu.VMEM((3 * modes, block), jnp.bfloat16),
            pltpu.VMEM((3 * modes, block), jnp.bfloat16),
            pltpu.VMEM((3 * modes, panels), jnp.float32),
            pltpu.VMEM((BLEND_DEPTH, block, panels), jnp.bfloat16),
            pltpu.SemaphoreType.DMA((BLEND_DEPTH,)),
            pltpu.VMEM(packed.shape, jnp.bfloat16),
            pltpu.SemaphoreType.DMA((PIECES,)),
        ],
        compiler_params=params(60),
        cost_estimate=pl.CostEstimate(
            flops=2 * 3 * modes * panels * slots,
            bytes_accessed=2 * panels * slots,
            transcendentals=0,
        ),
        name="moved_normals",
    )(index, packed, products, blend, normals)


def shards(

    displacement,
    send_index,
    support,
    support_xyz,
    patch_kernel_inverse,
    panel_xyz,
    normals,
    centers,
    member,
):
    axes = ("panel", "group")
    columns = displacement.shape[0]
    modes = columns // 3
    slots = send_index.shape[1]
    patches = centers.shape[1]
    support_count = slots // patches
    devices = lax.axis_size(axes)
    per = slots // devices
    own_rows = patch_kernel_inverse.shape[0]
    order = inverse_order(own_rows, support_count)
    if not np.array_equal(order, np.arange(support_count)):
        xyz = support_xyz.reshape(3, patches, support_count)
        support_xyz = jnp.take(xyz, order, axis=2).reshape(3, slots)

    groups = lax.axis_size("group")
    group = lax.axis_index("group")
    packs = [
        inverse_pack(patch_kernel_inverse, lax.rem(group + k, groups), patches)
        for k in range(groups)
    ]
    inverses = [packs[0]]
    for k in range(1, groups):
        ring = [(i, (i + k) % groups) for i in range(groups)]
        inverses.append(lax.ppermute(packs[k], "group", ring))
    outgoing = send_rows(displacement, send_index.reshape(slots), per)
    weights = panel_weights(panel_xyz, member, centers)
    outgoing, weights, inverses = lax.optimization_barrier((outgoing, weights, inverses))
    arriving = lax.all_to_all(
        outgoing.reshape(devices, per * 3 // 4, LANES), axes, 0, 0, tiled=True
    ).reshape(slots * 3 // 4, LANES)
    products = pair_products(group, inverses, support_count)
    blend = blend_entry_major(panel_xyz, weights, support_xyz, support_count)
    return moved_normals(
        support.reshape(slots), arriving, per, products, blend, normals, modes
    )


def solution(mesh):
    return jax.shard_map(
        shards,
        mesh=mesh,
        in_specs=(
            P(None, ("panel", "group")),
            P(("panel", "group"), None),
            P(("panel", "group"), None),
            P(None, ("panel", "group")),
            P("group", None, "panel"),
            P(None, ("panel", "group")),
            P(None, ("panel", "group")),
            P(None, ("panel", "group")),
            P(("panel", "group")),
        ),
        out_specs=P(None, ("panel", "group")),
        check_vma=False,
    )
```

```python
import functools

import jax
import jax.numpy as jnp
import numpy as np
from jax import lax
from jax.experimental import pallas as pl
from jax.experimental.pallas import tpu as pltpu
from jax.sharding import PartitionSpec as P

KERNEL_RADIUS = 0.45
ATTRACTION_REACH = 0.3
OWNER_PREMIUM = 8.0
LANES = 128
MIB = 1024 * 1024


def params(mib):
    return pltpu.CompilerParams(vmem_limit_bytes=mib * MIB)


def inverse_pack_kernel(window_ref, inverse_ref, out_ref):
    half = inverse_ref.shape[0] // 2
    for a in range(half):
        pair = jnp.concatenate([inverse_ref[a], inverse_ref[a + half]], axis=0)
        turned = pair.astype(jnp.float32).T
        out_ref[:, a * LANES : (a + 1) * LANES] = turned.astype(jnp.bfloat16)


def inverse_pack(inverse, window, patches):
    rows, support_count, _ = inverse.shape
    parts = patches // LANES
    width = rows * support_count
    return pl.pallas_call(
        inverse_pack_kernel,
        grid_spec=pltpu.PrefetchScalarGridSpec(
            num_scalar_prefetch=1,
            grid=(parts,),
            in_specs=[
                pl.BlockSpec(
                    (rows, support_count, LANES), lambda i, w: (0, 0, parts * w[0] + i)
                )
            ],
            out_specs=pl.BlockSpec((LANES, width), lambda i, w: (i, 0)),
        ),
        out_shape=jax.ShapeDtypeStruct((patches, width), jnp.bfloat16),
        compiler_params=params(24),
        cost_estimate=pl.CostEstimate(
            flops=0, bytes_accessed=4 * patches * width, transcendentals=0
        ),
        name="inverse_pack",
    )(window.reshape(1), inverse)


def inverse_order(rows, support_count):
    half = rows // 2
    order = []
    for v in range(support_count // 16):
        for side in range(2):
            for i in range(8):
                r = 8 * v + i
                order.append((r // half) * rows + side * half + r % half)
    return np.array(order)


UNROLL = 128
PIECES = 4


def gather_rows(index_ref, source, target, base, count):
    def body(step, carry):
        for r in range(UNROLL):
            at = step * UNROLL + r
            target[pl.ds(at, 1), :] = source[pl.ds(index_ref[base + at], 1), :]
        return carry

    lax.fori_loop(0, count // UNROLL, body, 0)


def send_kernel(
    per, index_ref, source_ref, out_ref, rows_ref, block_ref, displacement_ref, arrived
):
    columns, nodes = displacement_ref.shape
    piece_nodes = nodes // PIECES

    def fetch(i):
        span = pl.ds(i * piece_nodes, piece_nodes)
        return pltpu.make_async_copy(
            source_ref.at[:, span], displacement_ref.at[:, span], arrived.at[i]
        )

    for i in range(PIECES):
        fetch(i).start()

    def turn(block, carry):
        at = pl.multiple_of(block * LANES, LANES)
        piece = displacement_ref[:, pl.ds(at, LANES)].astype(jnp.float32)
        piece = jnp.concatenate([piece, piece[: LANES - columns]], axis=0)
        rows_ref[pl.ds(at, LANES), :] = piece.T
        return carry

    blocks = piece_nodes // LANES
    for i in range(PIECES):
        fetch(i).wait()
        lax.fori_loop(i * blocks, (i + 1) * blocks, turn, 0, unroll=4)
    quarter = per // 4
    lane = lax.broadcasted_iota(jnp.int32, (quarter, LANES), 1)

    def peer(d, carry):
        gather_rows(index_ref, rows_ref, block_ref, d * per, per)
        last = block_ref[3 * quarter : 4 * quarter, :]
        for i in range(3):
            own = block_ref[i * quarter : (i + 1) * quarter, :]
            full = jnp.where(lane < 96, own, pltpu.roll(last, 96 - 32 * i, 1))
            at = pl.multiple_of(d * 3 * quarter + i * quarter, quarter)
            out_ref[pl.ds(at, quarter), :] = full.astype(jnp.bfloat16)
        return carry

    lax.fori_loop(0, nodes // per, peer, 0)


def send_rows(displacement, index, per):
    columns, nodes = displacement.shape
    return pl.pallas_call(
        functools.partial(send_kernel, per),
        in_specs=[
            pl.BlockSpec(memory_space=pltpu.SMEM),
            pl.BlockSpec(memory_space=pl.ANY),
        ],
        out_specs=pl.BlockSpec(memory_space=pltpu.VMEM),
        out_shape=jax.ShapeDtypeStruct((nodes * 3 // 4, LANES), jnp.bfloat16),
        scratch_shapes=[
            pltpu.VMEM((nodes, LANES), jnp.float32),
            pltpu.VMEM((per, LANES), jnp.float32),
            pltpu.VMEM((columns, nodes), jnp.bfloat16),
            pltpu.SemaphoreType.DMA((PIECES,)),
        ],
        compiler_params=params(56),
        cost_estimate=pl.CostEstimate(
            flops=0, bytes_accessed=60 * MIB, transcendentals=0
        ),
        name="send_rows",
    )(index, displacement)


def unpack_rows(per, packed_ref, rows_ref):
    peers = rows_ref.shape[0] // per
    quarter = per // 4
    lane = lax.broadcasted_iota(jnp.int32, (quarter, LANES), 1)

    def peer(d, carry):
        parts = []
        for i in range(3):
            at = pl.multiple_of(d * 3 * quarter + i * quarter, quarter)
            piece = packed_ref[pl.ds(at, quarter), :].astype(jnp.float32)
            parts.append(pltpu.roll(piece, 32 * (i + 1), 1))
            to = pl.multiple_of(d * per + i * quarter, quarter)
            rows_ref[pl.ds(to, quarter), :] = piece
        last = jnp.where(lane < 32, parts[0], jnp.where(lane < 64, parts[1], parts[2]))
        to = pl.multiple_of(d * per + 3 * quarter, quarter)
        rows_ref[pl.ds(to, quarter), :] = last
        return carry

    lax.fori_loop(0, peers, peer, 0)


def splits(x):
    high = x.astype(jnp.bfloat16).astype(jnp.float32)
    rest = x - high
    middle = rest.astype(jnp.bfloat16).astype(jnp.float32)
    return high, middle, rest - middle


def distance_rows(xyz, entry_side):
    rows = []
    square = None
    for c in range(3):
        x = xyz[c : c + 1, :] * (1.0 / KERNEL_RADIUS)
        square = x * x if square is None else square + x * x
        if entry_side:
            s1, s2, s3 = splits(-2.0 * x)
            rows += [s1, s1, s2, s2, s1, s3]
        else:
            p1, p2, p3 = splits(x)
            rows += [p1, p2, p1, p2, p3, p1]
    one = jnp.ones_like(square)
    own = list(splits(square))
    rows += own + [one] * 3 if entry_side else [one] * 3 + own
    rows += [jnp.zeros_like(square)] * 8
    return jnp.concatenate(rows, axis=0)


def falloff_terms(scaled_sq):
    safe = jnp.maximum(scaled_sq, 1e-12)
    return jnp.maximum(1.0 - safe * lax.rsqrt(safe), 0.0)


PANEL_CHUNK = 2048


def weights_kernel(points_ref, member_ref, centers_ref, five_ref, four_ref):
    panels = points_ref.shape[1]
    patches = centers_ref.shape[0]
    patch = lax.broadcasted_iota(jnp.int32, (patches, LANES), 0)

    def weigh(b, carry):
        at = pl.multiple_of(b * LANES, LANES)
        square = None
        for c in range(3):
            gap = centers_ref[:, c : c + 1] - points_ref[c : c + 1, pl.ds(at, LANES)]
            square = gap * gap if square is None else square + gap * gap
        u = falloff_terms(square * (1.0 / ATTRACTION_REACH**2))
        u2 = u * u
        owner = jnp.where(member_ref[:, pl.ds(at, LANES)] == patch, OWNER_PREMIUM, 0.0)
        attraction = u2 * u2 * (5.0 - 4.0 * u) + owner
        weight = attraction / jnp.sum(attraction, axis=0, keepdims=True)
        five_ref[:, pl.ds(at, LANES)] = 5.0 * weight
        four_ref[:, pl.ds(at, LANES)] = 4.0 * weight
        return carry

    lax.fori_loop(0, panels // LANES, weigh, 0, unroll=2)


def panel_weights(points, member, centers):
    panels = points.shape[1]
    patches = centers.shape[1]
    tile = panels // 4
    shape = jax.ShapeDtypeStruct((patches, panels), jnp.float32)
    return pl.pallas_call(
        weights_kernel,
        grid=(panels // tile,),
        in_specs=[
            pl.BlockSpec((3, tile), lambda i: (0, i)),
            pl.BlockSpec((1, tile), lambda i: (0, i)),
            pl.BlockSpec((patches, 3), lambda i: (0, 0)),
        ],
        out_specs=[pl.BlockSpec((patches, tile), lambda i: (0, i))] * 2,
        out_shape=(shape, shape),
        compiler_params=params(60),
        cost_estimate=pl.CostEstimate(
            flops=20 * patches * panels,
            bytes_accessed=8 * patches * panels,
            transcendentals=patches * panels,
        ),
        name="panel_weights",
    )(points, member.reshape(1, panels), centers.T)


def blend_kernel(
    support_count, points_ref, five_ref, four_ref, support_ref, out_ref, panel_rows
):
    panels = points_ref.shape[1]
    block_patches = five_ref.shape[0]

    @pl.when(pl.program_id(0) == 0)
    def _():
        panel_rows[...] = distance_rows(points_ref[...], False).astype(jnp.bfloat16)

    entry_rows = distance_rows(support_ref[...], True).T.astype(jnp.bfloat16)

    def chunk(b, carry):
        at = pl.multiple_of(b * PANEL_CHUNK, PANEL_CHUNK)
        five = five_ref[:, pl.ds(at, PANEL_CHUNK)]
        four = four_ref[:, pl.ds(at, PANEL_CHUNK)]
        columns = panel_rows[:, pl.ds(at, PANEL_CHUNK)]
        whole = jnp.dot(entry_rows, columns, preferred_element_type=jnp.float32)
        for p in range(block_patches):
            rows = slice(p * support_count, (p + 1) * support_count)
            square = whole[rows]
            u = falloff_terms(square)
            u2 = u * u
            value = u2 * u2 * (five[p : p + 1] - four[p : p + 1] * u)
            out_ref[rows, pl.ds(at, PANEL_CHUNK)] = value.astype(jnp.bfloat16)
        return carry

    lax.fori_loop(0, panels // PANEL_CHUNK, chunk, 0)


def blend_entry_major(points, weights, support_xyz, support_count):
    panels = points.shape[1]
    slots = support_xyz.shape[1]
    block = 8 * support_count
    return pl.pallas_call(
        functools.partial(blend_kernel, support_count),
        grid=(slots // block,),
        in_specs=[
            pl.BlockSpec((3, panels), lambda i: (0, 0)),
            pl.BlockSpec((8, panels), lambda i: (i, 0)),
            pl.BlockSpec((8, panels), lambda i: (i, 0)),
            pl.BlockSpec((3, block), lambda i: (0, i)),
        ],
        out_specs=pl.BlockSpec((block, panels), lambda i: (i, 0)),
        out_shape=jax.ShapeDtypeStruct((slots, panels), jnp.bfloat16),
        scratch_shapes=[
            pltpu.VMEM((32, panels), jnp.bfloat16),
        ],
        compiler_params=params(60),
        cost_estimate=pl.CostEstimate(
            flops=64 * slots * panels,
            bytes_accessed=4 * slots * panels,
            transcendentals=slots * panels,
        ),
        name="blend",
    )(points, *weights, support_xyz)


BLOCK_PATCHES = 16
BLEND_DEPTH = 4
PRODUCT_PATCHES = 64


def products_kernel(support_count, groups, group_ref, *refs):
    inverse_refs = refs[:groups]
    out_ref, turned_ref = refs[groups:]
    block_patches, width = inverse_refs[0].shape
    halves = width // LANES
    per_patch = groups * halves
    for k in range(groups):
        owner = lax.rem(group_ref[0] + groups - k, groups)
        for a in range(halves):
            piece = inverse_refs[k][:, a * LANES : (a + 1) * LANES].astype(jnp.float32)
            turned_ref[pl.ds(owner * halves + a, block_patches, stride=per_patch), :] = piece
    lane = lax.broadcasted_iota(jnp.int32, (8, LANES), 1)
    low = lane < support_count
    for pair in range(block_patches // 2):
        rows = []
        for side in range(2):
            for v in range(per_patch // 8):
                at = (2 * pair + side) * per_patch + 8 * v
                own = turned_ref[at : at + 8, :]
                other = pltpu.roll(own, support_count, 1)
                both = (own, other) if side == 0 else (other, own)
                keep = low if side == 0 else jnp.logical_not(low)
                rows += [jnp.where(keep, x, 0.0) for x in both]
        product = jnp.concatenate(rows, axis=0).astype(jnp.bfloat16)
        out_ref[pair * LANES : (pair + 1) * LANES, :] = product


def pair_products(group, inverses, support_count):
    groups = len(inverses)
    patches, width = inverses[0].shape
    block = PRODUCT_PATCHES * support_count
    return pl.pallas_call(
        functools.partial(products_kernel, support_count, groups),
        grid=(patches // PRODUCT_PATCHES,),
        in_specs=[pl.BlockSpec(memory_space=pltpu.SMEM)]
        + [pl.BlockSpec((PRODUCT_PATCHES, width), lambda i: (i, 0))] * groups,
        out_specs=pl.BlockSpec((block, LANES), lambda i: (i, 0)),
        out_shape=jax.ShapeDtypeStruct((patches * support_count, LANES), jnp.bfloat16),
        scratch_shapes=[pltpu.VMEM((block // 2, LANES), jnp.float32)],
        compiler_params=params(60),
        cost_estimate=pl.CostEstimate(
            flops=0, bytes_accessed=20 * MIB, transcendentals=0
        ),
        name="pair_products",
    )(group.reshape(1), *inverses)


def moved_kernel(modes, per, index_ref, packed_ref, products_ref, blend_ref, normals_ref, *refs):
    out_ref, rows_ref, picked_ref, values_ref, coef_ref, summed_ref = refs[:6]
    total_ref, blend_slots, arrived = refs[6:]
    step = pl.program_id(0)
    steps = pl.num_programs(0) - 2
    block = picked_ref.shape[0]
    depth = blend_slots.shape[0]

    def fetch(b):
        return pltpu.make_async_copy(
            blend_ref.at[pl.ds(pl.multiple_of(b * block, block), block), :],
            blend_slots.at[lax.rem(b, depth)],
            arrived.at[lax.rem(b, depth)],
        )

    @pl.when(step == 0)
    def _():
        for b in range(depth):
            fetch(b).start()
        total_ref[...] = jnp.zeros_like(total_ref)
        values_ref[...] = jnp.zeros_like(values_ref)
        unpack_rows(per, packed_ref, rows_ref)

    @pl.when(step >= 2)
    def _():
        fetch(step - 2).wait()

        @pl.when(jnp.logical_and(step >= 3, step - 3 + depth < steps))
        def _():
            fetch(step - 3 + depth).start()

    slot = lax.rem(jnp.maximum(step - 2, 0), depth)
    base = jnp.minimum(step, steps - 1) * block
    pairs = block // LANES
    tile = total_ref.shape[1] // pairs

    def stages(summing, picking):
        if summing:
            summed_ref[...] = coef_ref[...]
        for pair in range(pairs):
            columns = slice(pair * tile, (pair + 1) * tile)
            if summing:
                total_ref[:, columns] += jnp.dot(
                    summed_ref[...],
                    blend_slots[slot, :, columns],
                    preferred_element_type=jnp.float32,
                )
            at = pair * LANES
            if picking:
                for r in range(at, at + LANES):
                    picked_ref[r : r + 1, :] = rows_ref[pl.ds(index_ref[base + r], 1), :]
            coef = jnp.dot(
                products_ref[at : at + LANES, :],
                values_ref[at : at + LANES, :],
                preferred_element_type=jnp.float32,
            )
            coef_ref[:, at : at + LANES] = coef.T[: 3 * modes].astype(jnp.bfloat16)
        if picking:
            values_ref[...] = picked_ref[...].astype(jnp.bfloat16)

    pl.when(step < 2)(lambda: stages(False, True))
    pl.when(jnp.logical_and(step >= 2, step < steps))(lambda: stages(True, True))
    pl.when(step >= steps)(lambda: stages(True, False))

    @pl.when(step == steps + 1)
    def _():
        result = None
        for c in range(3):
            term = normals_ref[c : c + 1, :] * total_ref[c * modes : (c + 1) * modes, :]
            result = term if result is None else result + term
        out_ref[...] = result


def moved_normals(index, packed, per, products, blend, normals, modes):
    slots, panels = blend.shape
    block = BLOCK_PATCHES * (LANES // 2)
    steps = slots // block

    def before(i):
        return jnp.clip(i - 1, 0, steps - 1)

    return pl.pallas_call(
        functools.partial(moved_kernel, modes, per),
        grid=(steps + 2,),
        in_specs=[
            pl.BlockSpec(memory_space=pltpu.SMEM),
            pl.BlockSpec(memory_space=pltpu.VMEM),
            pl.BlockSpec((block, LANES), lambda i: (before(i), 0)),
            pl.BlockSpec(memory_space=pl.ANY),
            pl.BlockSpec((3, panels), lambda i: (0, 0)),
        ],
        out_specs=pl.BlockSpec((modes, panels), lambda i: (0, 0)),
        out_shape=jax.ShapeDtypeStruct((modes, panels), jnp.float32),
        scratch_shapes=[
            pltpu.VMEM((slots, LANES), jnp.float32),
            pltpu.VMEM((block, LANES), jnp.float32),
            pltpu.VMEM((block, LANES), jnp.bfloat16),
            pltpu.VMEM((3 * modes, block), jnp.bfloat16),
            pltpu.VMEM((3 * modes, block), jnp.bfloat16),
            pltpu.VMEM((3 * modes, panels), jnp.float32),
            pltpu.VMEM((BLEND_DEPTH, block, panels), jnp.bfloat16),
            pltpu.SemaphoreType.DMA((BLEND_DEPTH,)),
        ],
        compiler_params=params(34),
        cost_estimate=pl.CostEstimate(
            flops=2 * 3 * modes * panels * slots,
            bytes_accessed=2 * panels * slots,
            transcendentals=0,
        ),
        name="moved_normals",
    )(index, packed, products, blend, normals)


def shards(

    displacement,
    send_index,
    support,
    support_xyz,
    patch_kernel_inverse,
    panel_xyz,
    normals,
    centers,
    member,
):
    axes = ("panel", "group")
    columns = displacement.shape[0]
    modes = columns // 3
    slots = send_index.shape[1]
    patches = centers.shape[1]
    support_count = slots // patches
    devices = lax.axis_size(axes)
    per = slots // devices
    own_rows = patch_kernel_inverse.shape[0]
    order = inverse_order(own_rows, support_count)
    if not np.array_equal(order, np.arange(support_count)):
        xyz = support_xyz.reshape(3, patches, support_count)
        support_xyz = jnp.take(xyz, order, axis=2).reshape(3, slots)

    groups = lax.axis_size("group")
    group = lax.axis_index("group")
    packs = [
        inverse_pack(patch_kernel_inverse, lax.rem(group + k, groups), patches)
        for k in range(groups)
    ]
    inverses = [packs[0]]
    for k in range(1, groups):
        ring = [(i, (i + k) % groups) for i in range(groups)]
        inverses.append(lax.ppermute(packs[k], "group", ring))
    outgoing = send_rows(displacement, send_index.reshape(slots), per)
    weights = panel_weights(panel_xyz, member, centers)
    outgoing, weights, inverses = lax.optimization_barrier((outgoing, weights, inverses))
    arriving = lax.all_to_all(
        outgoing.reshape(devices, per * 3 // 4, LANES), axes, 0, 0, tiled=True
    ).reshape(slots * 3 // 4, LANES)
    products = pair_products(group, inverses, support_count)
    blend = blend_entry_major(panel_xyz, weights, support_xyz, support_count)
    return moved_normals(
        support.reshape(slots), arriving, per, products, blend, normals, modes
    )


def solution(mesh):
    return jax.shard_map(
        shards,
        mesh=mesh,
        in_specs=(
            P(None, ("panel", "group")),
            P(("panel", "group"), None),
            P(("panel", "group"), None),
            P(None, ("panel", "group")),
            P("group", None, "panel"),
            P(None, ("panel", "group")),
            P(None, ("panel", "group")),
            P(None, ("panel", "group")),
            P(("panel", "group")),
        ),
        out_specs=P(None, ("panel", "group")),
        check_vma=False,
    )
```

```python
import functools

import jax
import jax.numpy as jnp
import numpy as np
from jax import lax
from jax.experimental import pallas as pl
from jax.experimental.pallas import tpu as pltpu
from jax.sharding import PartitionSpec as P

KERNEL_RADIUS = 0.45
ATTRACTION_REACH = 0.3
OWNER_PREMIUM = 8.0
LANES = 128
MIB = 1024 * 1024


def params(mib):
    return pltpu.CompilerParams(vmem_limit_bytes=mib * MIB)


def inverse_pack_kernel(window_ref, inverse_ref, out_ref):
    half = inverse_ref.shape[0] // 2
    for a in range(half):
        pair = jnp.concatenate([inverse_ref[a], inverse_ref[a + half]], axis=0)
        turned = pair.astype(jnp.float32).T
        out_ref[:, a * LANES : (a + 1) * LANES] = turned.astype(jnp.bfloat16)


def inverse_pack(inverse, window, patches):
    rows, support_count, _ = inverse.shape
    parts = patches // LANES
    width = rows * support_count
    return pl.pallas_call(
        inverse_pack_kernel,
        grid_spec=pltpu.PrefetchScalarGridSpec(
            num_scalar_prefetch=1,
            grid=(parts,),
            in_specs=[
                pl.BlockSpec(
                    (rows, support_count, LANES), lambda i, w: (0, 0, parts * w[0] + i)
                )
            ],
            out_specs=pl.BlockSpec((LANES, width), lambda i, w: (i, 0)),
        ),
        out_shape=jax.ShapeDtypeStruct((patches, width), jnp.bfloat16),
        compiler_params=params(24),
        cost_estimate=pl.CostEstimate(
            flops=0, bytes_accessed=4 * patches * width, transcendentals=0
        ),
        name="inverse_pack",
    )(window.reshape(1), inverse)


def inverse_order(rows, support_count):
    half = rows // 2
    order = []
    for v in range(support_count // 16):
        for side in range(2):
            for i in range(8):
                r = 8 * v + i
                order.append((r // half) * rows + side * half + r % half)
    return np.array(order)


UNROLL = 128
PIECES = 4


def gather_rows(index_ref, source, target, base, count):
    def body(step, carry):
        for r in range(UNROLL):
            at = step * UNROLL + r
            target[pl.ds(at, 1), :] = source[pl.ds(index_ref[base + at], 1), :]
        return carry

    lax.fori_loop(0, count // UNROLL, body, 0)


def send_kernel(
    per, index_ref, source_ref, out_ref, rows_ref, block_ref, displacement_ref, arrived
):
    columns, nodes = displacement_ref.shape
    piece_nodes = nodes // PIECES

    def fetch(i):
        span = pl.ds(i * piece_nodes, piece_nodes)
        return pltpu.make_async_copy(
            source_ref.at[:, span], displacement_ref.at[:, span], arrived.at[i]
        )

    for i in range(PIECES):
        fetch(i).start()

    def turn(block, carry):
        at = pl.multiple_of(block * LANES, LANES)
        piece = displacement_ref[:, pl.ds(at, LANES)].astype(jnp.float32)
        piece = jnp.concatenate([piece, piece[: LANES - columns]], axis=0)
        rows_ref[pl.ds(at, LANES), :] = piece.T
        return carry

    blocks = piece_nodes // LANES
    for i in range(PIECES):
        fetch(i).wait()
        lax.fori_loop(i * blocks, (i + 1) * blocks, turn, 0, unroll=4)
    quarter = per // 4
    lane = lax.broadcasted_iota(jnp.int32, (quarter, LANES), 1)

    def peer(d, carry):
        gather_rows(index_ref, rows_ref, block_ref, d * per, per)
        last = block_ref[3 * quarter : 4 * quarter, :]
        for i in range(3):
            own = block_ref[i * quarter : (i + 1) * quarter, :]
            full = jnp.where(lane < 96, own, pltpu.roll(last, 96 - 32 * i, 1))
            at = pl.multiple_of(d * 3 * quarter + i * quarter, quarter)
            out_ref[pl.ds(at, quarter), :] = full.astype(jnp.bfloat16)
        return carry

    lax.fori_loop(0, nodes // per, peer, 0)


def send_rows(displacement, index, per):
    columns, nodes = displacement.shape
    return pl.pallas_call(
        functools.partial(send_kernel, per),
        in_specs=[
            pl.BlockSpec(memory_space=pltpu.SMEM),
            pl.BlockSpec(memory_space=pl.ANY),
        ],
        out_specs=pl.BlockSpec(memory_space=pltpu.VMEM),
        out_shape=jax.ShapeDtypeStruct((nodes * 3 // 4, LANES), jnp.bfloat16),
        scratch_shapes=[
            pltpu.VMEM((nodes, LANES), jnp.float32),
            pltpu.VMEM((per, LANES), jnp.float32),
            pltpu.VMEM((columns, nodes), jnp.bfloat16),
            pltpu.SemaphoreType.DMA((PIECES,)),
        ],
        compiler_params=params(56),
        cost_estimate=pl.CostEstimate(
            flops=0, bytes_accessed=60 * MIB, transcendentals=0
        ),
        name="send_rows",
    )(index, displacement)


def unpack_rows(per, packed_ref, rows_ref):
    peers = rows_ref.shape[0] // per
    quarter = per // 4
    lane = lax.broadcasted_iota(jnp.int32, (quarter, LANES), 1)

    def peer(d, carry):
        parts = []
        for i in range(3):
            at = pl.multiple_of(d * 3 * quarter + i * quarter, quarter)
            piece = packed_ref[pl.ds(at, quarter), :].astype(jnp.float32)
            parts.append(pltpu.roll(piece, 32 * (i + 1), 1))
            to = pl.multiple_of(d * per + i * quarter, quarter)
            rows_ref[pl.ds(to, quarter), :] = piece
        last = jnp.where(lane < 32, parts[0], jnp.where(lane < 64, parts[1], parts[2]))
        to = pl.multiple_of(d * per + 3 * quarter, quarter)
        rows_ref[pl.ds(to, quarter), :] = last
        return carry

    lax.fori_loop(0, peers, peer, 0)


def splits(x):
    high = x.astype(jnp.bfloat16).astype(jnp.float32)
    rest = x - high
    middle = rest.astype(jnp.bfloat16).astype(jnp.float32)
    return high, middle, rest - middle


def distance_rows(xyz, entry_side):
    rows = []
    square = None
    for c in range(3):
        x = xyz[c : c + 1, :] * (1.0 / KERNEL_RADIUS)
        square = x * x if square is None else square + x * x
        if entry_side:
            s1, s2, s3 = splits(-2.0 * x)
            rows += [s1, s1, s2, s2, s1, s3]
        else:
            p1, p2, p3 = splits(x)
            rows += [p1, p2, p1, p2, p3, p1]
    one = jnp.ones_like(square)
    own = list(splits(square))
    rows += own + [one] * 3 if entry_side else [one] * 3 + own
    rows += [jnp.zeros_like(square)] * 8
    return jnp.concatenate(rows, axis=0)


def falloff_terms(scaled_sq):
    safe = jnp.maximum(scaled_sq, 1e-12)
    return jnp.maximum(1.0 - safe * lax.rsqrt(safe), 0.0)


PANEL_CHUNK = 2048


def weights_kernel(points_ref, member_ref, centers_ref, five_ref, four_ref):
    panels = points_ref.shape[1]
    patches = centers_ref.shape[0]
    patch = lax.broadcasted_iota(jnp.int32, (patches, LANES), 0)

    def weigh(b, carry):
        at = pl.multiple_of(b * LANES, LANES)
        square = None
        for c in range(3):
            gap = centers_ref[:, c : c + 1] - points_ref[c : c + 1, pl.ds(at, LANES)]
            square = gap * gap if square is None else square + gap * gap
        u = falloff_terms(square * (1.0 / ATTRACTION_REACH**2))
        u2 = u * u
        owner = jnp.where(member_ref[:, pl.ds(at, LANES)] == patch, OWNER_PREMIUM, 0.0)
        attraction = u2 * u2 * (5.0 - 4.0 * u) + owner
        weight = attraction / jnp.sum(attraction, axis=0, keepdims=True)
        five_ref[:, pl.ds(at, LANES)] = 5.0 * weight
        four_ref[:, pl.ds(at, LANES)] = 4.0 * weight
        return carry

    lax.fori_loop(0, panels // LANES, weigh, 0, unroll=2)


def panel_weights(points, member, centers):
    panels = points.shape[1]
    patches = centers.shape[1]
    tile = panels // 4
    shape = jax.ShapeDtypeStruct((patches, panels), jnp.float32)
    return pl.pallas_call(
        weights_kernel,
        grid=(panels // tile,),
        in_specs=[
            pl.BlockSpec((3, tile), lambda i: (0, i)),
            pl.BlockSpec((1, tile), lambda i: (0, i)),
            pl.BlockSpec((patches, 3), lambda i: (0, 0)),
        ],
        out_specs=[pl.BlockSpec((patches, tile), lambda i: (0, i))] * 2,
        out_shape=(shape, shape),
        compiler_params=params(60),
        cost_estimate=pl.CostEstimate(
            flops=20 * patches * panels,
            bytes_accessed=8 * patches * panels,
            transcendentals=patches * panels,
        ),
        name="panel_weights",
    )(points, member.reshape(1, panels), centers.T)


def blend_kernel(
    support_count, points_ref, five_ref, four_ref, support_ref, out_ref, panel_rows
):
    panels = points_ref.shape[1]
    block_patches = five_ref.shape[0]

    @pl.when(pl.program_id(0) == 0)
    def _():
        panel_rows[...] = distance_rows(points_ref[...], False).astype(jnp.bfloat16)

    entry_rows = distance_rows(support_ref[...], True).T.astype(jnp.bfloat16)

    def chunk(b, carry):
        at = pl.multiple_of(b * PANEL_CHUNK, PANEL_CHUNK)
        five = five_ref[:, pl.ds(at, PANEL_CHUNK)]
        four = four_ref[:, pl.ds(at, PANEL_CHUNK)]
        columns = panel_rows[:, pl.ds(at, PANEL_CHUNK)]
        whole = jnp.dot(entry_rows, columns, preferred_element_type=jnp.float32)
        for p in range(block_patches):
            rows = slice(p * support_count, (p + 1) * support_count)
            square = whole[rows]
            u = falloff_terms(square)
            u2 = u * u
            value = u2 * u2 * (five[p : p + 1] - four[p : p + 1] * u)
            out_ref[rows, pl.ds(at, PANEL_CHUNK)] = value.astype(jnp.bfloat16)
        return carry

    lax.fori_loop(0, panels // PANEL_CHUNK, chunk, 0)


def blend_entry_major(points, weights, support_xyz, support_count):
    panels = points.shape[1]
    slots = support_xyz.shape[1]
    block = 16 * support_count
    return pl.pallas_call(
        functools.partial(blend_kernel, support_count),
        grid=(slots // block,),
        in_specs=[
            pl.BlockSpec((3, panels), lambda i: (0, 0)),
            pl.BlockSpec((16, panels), lambda i: (i, 0)),
            pl.BlockSpec((16, panels), lambda i: (i, 0)),
            pl.BlockSpec((3, block), lambda i: (0, i)),
        ],
        out_specs=pl.BlockSpec((block, panels), lambda i: (i, 0)),
        out_shape=jax.ShapeDtypeStruct((slots, panels), jnp.bfloat16),
        scratch_shapes=[
            pltpu.VMEM((32, panels), jnp.bfloat16),
        ],
        compiler_params=params(60),
        cost_estimate=pl.CostEstimate(
            flops=64 * slots * panels,
            bytes_accessed=4 * slots * panels,
            transcendentals=slots * panels,
        ),
        name="blend",
    )(points, *weights, support_xyz)


BLOCK_PATCHES = 16
BLEND_DEPTH = 4
PRODUCT_PATCHES = 128


def products_kernel(support_count, groups, group_ref, *refs):
    inverse_refs = refs[:groups]
    out_ref, turned_ref = refs[groups:]
    block_patches, width = inverse_refs[0].shape
    halves = width // LANES
    per_patch = groups * halves
    for k in range(groups):
        owner = lax.rem(group_ref[0] + groups - k, groups)
        for a in range(halves):
            piece = inverse_refs[k][:, a * LANES : (a + 1) * LANES].astype(jnp.float32)
            turned_ref[pl.ds(owner * halves + a, block_patches, stride=per_patch), :] = piece
    lane = lax.broadcasted_iota(jnp.int32, (8, LANES), 1)
    low = lane < support_count
    for pair in range(block_patches // 2):
        rows = []
        for side in range(2):
            for v in range(per_patch // 8):
                at = (2 * pair + side) * per_patch + 8 * v
                own = turned_ref[at : at + 8, :]
                other = pltpu.roll(own, support_count, 1)
                both = (own, other) if side == 0 else (other, own)
                keep = low if side == 0 else jnp.logical_not(low)
                rows += [jnp.where(keep, x, 0.0) for x in both]
        product = jnp.concatenate(rows, axis=0).astype(jnp.bfloat16)
        out_ref[pair * LANES : (pair + 1) * LANES, :] = product


def pair_products(group, inverses, support_count):
    groups = len(inverses)
    patches, width = inverses[0].shape
    block = PRODUCT_PATCHES * support_count
    return pl.pallas_call(
        functools.partial(products_kernel, support_count, groups),
        grid=(patches // PRODUCT_PATCHES,),
        in_specs=[pl.BlockSpec(memory_space=pltpu.SMEM)]
        + [pl.BlockSpec((PRODUCT_PATCHES, width), lambda i: (i, 0))] * groups,
        out_specs=pl.BlockSpec((block, LANES), lambda i: (i, 0)),
        out_shape=jax.ShapeDtypeStruct((patches * support_count, LANES), jnp.bfloat16),
        scratch_shapes=[pltpu.VMEM((block // 2 + LANES, LANES), jnp.float32)],
        compiler_params=params(60),
        cost_estimate=pl.CostEstimate(
            flops=0, bytes_accessed=20 * MIB, transcendentals=0
        ),
        name="pair_products",
    )(group.reshape(1), *inverses)


def moved_kernel(modes, per, index_ref, packed_ref, products_ref, blend_ref, normals_ref, *refs):
    out_ref, rows_ref, picked_ref, values_ref, coef_ref, summed_ref = refs[:6]
    total_ref, blend_slots, arrived = refs[6:]
    step = pl.program_id(0)
    steps = pl.num_programs(0) - 2
    block = picked_ref.shape[0]
    depth = blend_slots.shape[0]

    def fetch(b):
        return pltpu.make_async_copy(
            blend_ref.at[pl.ds(pl.multiple_of(b * block, block), block), :],
            blend_slots.at[lax.rem(b, depth)],
            arrived.at[lax.rem(b, depth)],
        )

    @pl.when(step == 0)
    def _():
        for b in range(depth):
            fetch(b).start()
        total_ref[...] = jnp.zeros_like(total_ref)
        values_ref[...] = jnp.zeros_like(values_ref)
        unpack_rows(per, packed_ref, rows_ref)

    @pl.when(step >= 2)
    def _():
        fetch(step - 2).wait()

        @pl.when(jnp.logical_and(step >= 3, step - 3 + depth < steps))
        def _():
            fetch(step - 3 + depth).start()

    slot = lax.rem(jnp.maximum(step - 2, 0), depth)
    base = jnp.minimum(step, steps - 1) * block
    pairs = block // LANES
    tile = total_ref.shape[1] // pairs

    def stages(summing, picking):
        if summing:
            summed_ref[...] = coef_ref[...]
        for pair in range(pairs):
            columns = slice(pair * tile, (pair + 1) * tile)
            if summing:
                total_ref[:, columns] += jnp.dot(
                    summed_ref[...],
                    blend_slots[slot, :, columns],
                    preferred_element_type=jnp.float32,
                )
            at = pair * LANES
            if picking:
                for r in range(at, at + LANES):
                    picked_ref[r : r + 1, :] = rows_ref[pl.ds(index_ref[base + r], 1), :]
            coef = jnp.dot(
                products_ref[at : at + LANES, :],
                values_ref[at : at + LANES, :],
                preferred_element_type=jnp.float32,
            )
            coef_ref[:, at : at + LANES] = coef.T[: 3 * modes].astype(jnp.bfloat16)
        if picking:
            values_ref[...] = picked_ref[...].astype(jnp.bfloat16)

    pl.when(step < 2)(lambda: stages(False, True))
    pl.when(jnp.logical_and(step >= 2, step < steps))(lambda: stages(True, True))
    pl.when(step >= steps)(lambda: stages(True, False))

    @pl.when(step == steps + 1)
    def _():
        result = None
        for c in range(3):
            term = normals_ref[c : c + 1, :] * total_ref[c * modes : (c + 1) * modes, :]
            result = term if result is None else result + term
        out_ref[...] = result


def moved_normals(index, packed, per, products, blend, normals, modes):
    slots, panels = blend.shape
    block = BLOCK_PATCHES * (LANES // 2)
    steps = slots // block

    def before(i):
        return jnp.clip(i - 1, 0, steps - 1)

    return pl.pallas_call(
        functools.partial(moved_kernel, modes, per),
        grid=(steps + 2,),
        in_specs=[
            pl.BlockSpec(memory_space=pltpu.SMEM),
            pl.BlockSpec(memory_space=pltpu.VMEM),
            pl.BlockSpec((block, LANES), lambda i: (before(i), 0)),
            pl.BlockSpec(memory_space=pl.ANY),
            pl.BlockSpec((3, panels), lambda i: (0, 0)),
        ],
        out_specs=pl.BlockSpec((modes, panels), lambda i: (0, 0)),
        out_shape=jax.ShapeDtypeStruct((modes, panels), jnp.float32),
        scratch_shapes=[
            pltpu.VMEM((slots, LANES), jnp.float32),
            pltpu.VMEM((block, LANES), jnp.float32),
            pltpu.VMEM((block, LANES), jnp.bfloat16),
            pltpu.VMEM((3 * modes, block), jnp.bfloat16),
            pltpu.VMEM((3 * modes, block), jnp.bfloat16),
            pltpu.VMEM((3 * modes, panels), jnp.float32),
            pltpu.VMEM((BLEND_DEPTH, block, panels), jnp.bfloat16),
            pltpu.SemaphoreType.DMA((BLEND_DEPTH,)),
        ],
        compiler_params=params(34),
        cost_estimate=pl.CostEstimate(
            flops=2 * 3 * modes * panels * slots,
            bytes_accessed=2 * panels * slots,
            transcendentals=0,
        ),
        name="moved_normals",
    )(index, packed, products, blend, normals)


def shards(

    displacement,
    send_index,
    support,
    support_xyz,
    patch_kernel_inverse,
    panel_xyz,
    normals,
    centers,
    member,
):
    axes = ("panel", "group")
    columns = displacement.shape[0]
    modes = columns // 3
    slots = send_index.shape[1]
    patches = centers.shape[1]
    support_count = slots // patches
    devices = lax.axis_size(axes)
    per = slots // devices
    own_rows = patch_kernel_inverse.shape[0]
    order = inverse_order(own_rows, support_count)
    if not np.array_equal(order, np.arange(support_count)):
        xyz = support_xyz.reshape(3, patches, support_count)
        support_xyz = jnp.take(xyz, order, axis=2).reshape(3, slots)

    groups = lax.axis_size("group")
    group = lax.axis_index("group")
    packs = [
        inverse_pack(patch_kernel_inverse, lax.rem(group + k, groups), patches)
        for k in range(groups)
    ]
    inverses = [packs[0]]
    for k in range(1, groups):
        ring = [(i, (i + k) % groups) for i in range(groups)]
        inverses.append(lax.ppermute(packs[k], "group", ring))
    outgoing = send_rows(displacement, send_index.reshape(slots), per)
    weights = panel_weights(panel_xyz, member, centers)
    outgoing, weights, inverses = lax.optimization_barrier((outgoing, weights, inverses))
    arriving = lax.all_to_all(
        outgoing.reshape(devices, per * 3 // 4, LANES), axes, 0, 0, tiled=True
    ).reshape(slots * 3 // 4, LANES)
    products = pair_products(group, inverses, support_count)
    blend = blend_entry_major(panel_xyz, weights, support_xyz, support_count)
    return moved_normals(
        support.reshape(slots), arriving, per, products, blend, normals, modes
    )


def solution(mesh):
    return jax.shard_map(
        shards,
        mesh=mesh,
        in_specs=(
            P(None, ("panel", "group")),
            P(("panel", "group"), None),
            P(("panel", "group"), None),
            P(None, ("panel", "group")),
            P("group", None, "panel"),
            P(None, ("panel", "group")),
            P(None, ("panel", "group")),
            P(None, ("panel", "group")),
            P(("panel", "group")),
        ),
        out_specs=P(None, ("panel", "group")),
        check_vma=False,
    )
```
